128 devices in a mesh: pipe: 2 (over core), dp: 4 (over y), tensor: 16 (over z, x).
Axes of the slice: x: 4, y: 4, z: 4, core: 2. Of those that a mesh axis runs over, the one named last changes fastest.
Arguments:
- tokens: bfloat16 [2, 1024, 1536], P(None, 'dp'), may hold values from -6 to 6
- seq_lengths: int32 [2, 2], replicated, may hold values from 1 to 769, 1024 in all within a row
- cotangent: bfloat16 [2, 1024, 1536], P(None, 'dp'), may hold values from -6 to 6
- pre_gain: float32 [2, 1536], P('pipe'), may hold values from 0.1 to 1.9
- w_z: bfloat16 [2, 1536, 3072], P('pipe', None, 'tensor'), may hold values from -0.15625 to 0.15625
- w_x: bfloat16 [2, 1536, 3072], P('pipe', None, 'tensor'), may hold values from -0.15625 to 0.15625
- w_bc: bfloat16 [2, 1536, 256], P('pipe'), may hold values from -0.15625 to 0.15625
- w_dt: bfloat16 [2, 1536, 48], P('pipe', None, 'tensor'), may hold values from -0.15625 to 0.15625
- conv_x: float32 [2, 4, 3072], P('pipe', None, 'tensor'), may hold values from -3 to 3
- conv_bc: float32 [2, 4, 256], P('pipe'), may hold values from -3 to 3
- conv_bias_x: float32 [2, 3072], P('pipe', 'tensor'), may hold values from -0.5 to 0.5
- conv_bias_bc: float32 [2, 256], P('pipe'), may hold values from -0.5 to 0.5
- dt_bias: float32 [2, 48], P('pipe', 'tensor'), may hold values from -3 to -1
- a_log: float32 [2, 48], P('pipe', 'tensor'), may hold values from -8 to -2
- d_skip: float32 [2, 48], P('pipe', 'tensor'), may hold values from 0.5 to 1.5
- inner_gain: float32 [2, 3072], P('pipe', 'tensor'), may hold values from 0.1 to 1.9
- w_out: bfloat16 [2, 3072, 1536], P('pipe', 'tensor'), may hold values from -0.109375 to 0.109375
Outputs:
- section_outputs: bfloat16 [2, 2, 1024, 1536], P('pipe', None, 'dp')
- input_grads: bfloat16 [2, 2, 1024, 1536], P('pipe', None, 'dp')
- grad_pre_gain: float32 [2, 1536], P('pipe')
- grad_w_z: float32 [2, 1536, 3072], P('pipe', None, 'tensor')
- grad_w_x: float32 [2, 1536, 3072], P('pipe', None, 'tensor')
- grad_w_bc: float32 [2, 1536, 256], P('pipe')
- grad_w_dt: float32 [2, 1536, 48], P('pipe', None, 'tensor')
- grad_conv_x: float32 [2, 4, 3072], P('pipe', None, 'tensor')
- grad_conv_bc: float32 [2, 4, 256], P('pipe')
- grad_conv_bias_x: float32 [2, 3072], P('pipe', 'tensor')
- grad_conv_bias_bc: float32 [2, 256], P('pipe')
- grad_dt_bias: float32 [2, 48], P('pipe', 'tensor')
- grad_a_log: float32 [2, 48], P('pipe', 'tensor')
- grad_d_skip: float32 [2, 48], P('pipe', 'tensor')
- grad_inner_gain: float32 [2, 3072], P('pipe', 'tensor')
- grad_w_out: float32 [2, 3072, 1536], P('pipe', 'tensor')
The draws below stay inside these ranges and needn't reach their ends.
Inputs may be any that keep to these rules, and one draw needn't show every extreme that they name: `seq_lengths`: each row sums to 1024; its longest sequence has at most 769 tokens.
All inputs are finite; a program needn't handle non-finite values.
Results may differ from the reference program's by a relative error of at most 0.019.
Values may be sent and summed in bfloat16 or wider, within the bound.
A program may use at most 128 MiB of HBM per device.

```python
import math
import jax
import jax.numpy as jnp
import numpy as np
from jax import lax

D = 1536
HEADS = 48
HEADDIM = 64
STATE = 128
CONV = 4
GROUP = 128
MICRO = 2
NSEQ = 2
INNER = 3072
MB_TOK = 1024
LONGEST = 769
SECTIONS = 2


def block_levels(rng, extent, shards, least, top_value):
    gain, own = 1.0, jax.random.fold_in(rng, 6)
    for position, blocks in shards:
        heights = jnp.exp(jax.random.uniform(jax.random.fold_in(own, position), (blocks,), jnp.float32, least / len(shards), top_value / len(shards)))
        gain = gain * jnp.repeat(heights, extent[position] // blocks).reshape([-1 if axis == position else 1 for axis in range(len(extent))])
    return gain


def profile(count, total, bound, lean):
    portions = [(1 << 20) // math.isqrt(rank ** lean) + 1 for rank in range(2, count + 1)]
    rest, holding = total - bound - (count - 1), [1] * (count - 1)
    while rest > 0:
        candidates = [i for i in range(count - 1) if holding[i] < bound]
        pool, remaining = sum([portions[i] for i in candidates]), rest
        for i in candidates:
            extra = min(bound - holding[i], max(1, remaining * portions[i] // pool), rest)
            holding[i] = holding[i] + extra
            rest = rest - extra
    return np.array([bound] + holding)


def uneven(stream_key, number_of, total, most, lean):
    if number_of == 2:
        one = jax.random.randint(stream_key, (), max(1, total - most), min(most, total - 1) + 1)
        return jnp.stack([one, total - one])
    sizes = jnp.asarray(profile(number_of, total, most, lean), jnp.int32)
    couples = (number_of - 1) // 2
    donor, receiver = sizes[1:1 + 2 * couples:2], sizes[2:2 + 2 * couples:2]
    slack = jnp.minimum(donor - 1, most - receiver)
    moved = jax.random.randint(jax.random.fold_in(stream_key, 1), (couples,), 0, 1 << 20) % (slack + 1)
    sizes = sizes.at[1:1 + 2 * couples:2].set(donor - moved).at[2:2 + 2 * couples:2].set(receiver + moved)
    return sizes[jax.random.permutation(jax.random.fold_in(stream_key, 2), number_of)]


def bell_draw(own_key, shape, spread, reach, cuts=(), held_as=jnp.bfloat16):
    result = jax.random.normal(own_key, shape, jnp.float32) * spread
    if len(cuts) > 0:
        result = block_levels(own_key, shape, cuts, -0.22, 0.18) * result
    return jnp.clip(result, min=-reach, max=reach).astype(held_as)


def setup_inputs(seed: int = 0) -> dict:
    keys = jax.random.split(jax.random.key(seed), 18)
    tokens = bell_draw(keys[0], (MICRO, MB_TOK, D), 1.0, 6.0, ((1, 4),))
    seq_lengths = jax.vmap(lambda own: uneven(own, NSEQ, MB_TOK, LONGEST, 1))(jax.random.split(keys[1], MICRO)).reshape((MICRO, NSEQ)).astype(jnp.int32)
    cotangent = bell_draw(keys[2], (MICRO, MB_TOK, D), 1.0, 6.0, ((1, 4),))
    pre_gain = jnp.clip(1.0 + 0.18 * jax.random.normal(keys[3], (SECTIONS, D), jnp.float32), 0.1, 1.9)
    w_z = bell_draw(keys[4], (SECTIONS, D, INNER), D ** -0.5, 0.15625, ((0, 2), (2, 16)))
    w_x = bell_draw(keys[5], (SECTIONS, D, INNER), D ** -0.5, 0.15625, ((0, 2), (2, 16)))
    w_bc = bell_draw(keys[6], (SECTIONS, D, 2 * STATE), D ** -0.5, 0.15625, ((0, 2),))
    w_dt = bell_draw(keys[7], (SECTIONS, D, HEADS), D ** -0.5, 0.15625, ((0, 2), (2, 16)))
    conv_x = bell_draw(keys[8], (SECTIONS, CONV, INNER), 0.5, 3.0, ((0, 2), (2, 16)), jnp.float32)
    conv_bc = bell_draw(keys[9], (SECTIONS, CONV, 2 * STATE), 0.5, 3.0, ((0, 2),), jnp.float32)
    conv_bias_x = jnp.clip(jax.random.uniform(keys[10], (SECTIONS, INNER), jnp.float32, -0.5, 0.5) * block_levels(keys[10], (SECTIONS, INNER), ((0, 2), (1, 16)), -0.4, 0.0), -0.5, 0.5)
    conv_bias_bc = jnp.clip(jax.random.uniform(keys[11], (SECTIONS, 2 * STATE), jnp.float32, -0.5, 0.5) * block_levels(keys[11], (SECTIONS, 2 * STATE), ((0, 2),), -0.4, 0.0), -0.5, 0.5)
    dt_bias = jnp.clip(-3.0 + 2.0 * jax.random.uniform(keys[12], (SECTIONS, HEADS), jnp.float32) ** block_levels(keys[12], (SECTIONS, HEADS), ((0, 2), (1, 16)), -0.2, 0.2), -3.0, -1.0)
    a_log = jnp.clip(-8.0 + 6.0 * jax.random.uniform(keys[13], (SECTIONS, HEADS), jnp.float32) ** block_levels(keys[13], (SECTIONS, HEADS), ((0, 2), (1, 16)), -0.2, 0.2), -8.0, -2.0)
    d_skip = jnp.clip(0.5 + 1.0 * jax.random.uniform(keys[14], (SECTIONS, HEADS), jnp.float32) ** block_levels(keys[14], (SECTIONS, HEADS), ((0, 2), (1, 16)), -0.2, 0.2), 0.5, 1.5)
    inner_gain = jnp.clip(1.0 + 0.18 * jax.random.normal(keys[15], (SECTIONS, INNER), jnp.float32), 0.1, 1.9)
    w_out = bell_draw(keys[16], (SECTIONS, INNER, D), INNER ** -0.5, 0.109375, ((0, 2), (1, 16)))
    return {"tokens": tokens, "seq_lengths": seq_lengths, "cotangent": cotangent, "pre_gain": pre_gain, "w_z": w_z, "w_x": w_x, "w_bc": w_bc, "w_dt": w_dt, "conv_x": conv_x, "conv_bc": conv_bc, "conv_bias_x": conv_bias_x, "conv_bias_bc": conv_bias_bc, "dt_bias": dt_bias, "a_log": a_log, "d_skip": d_skip, "inner_gain": inner_gain, "w_out": w_out}


@jax.custom_vjp
def low(v):
    return lax.optimization_barrier(v.astype(jnp.bfloat16)).astype(jnp.float32)

@jax.custom_vjp
def low_back(v):
    return v

def low_keep(v):
    return (low(v), None)

def low_pass(kept, grad):
    return (grad,)

def back_keep(v):
    return (v, None)

def back_low(kept, grad):
    return (low(grad),)
low.defvjp(low_keep, low_pass)
low_back.defvjp(back_keep, back_low)
highest = lax.Precision.HIGHEST
epsilon = 1e-05

def silu_act(signal):
    return signal * jax.nn.sigmoid(signal)

def sequence_ids(seq_lengths, positions):
    seq_ends = jnp.cumsum(seq_lengths, dtype=jnp.int32).astype(jnp.int32)
    counted = lax.optimization_barrier(jnp.sum((positions[:, None] >= seq_ends[None, :]).astype(jnp.int32), axis=1, dtype=jnp.int32))
    return jnp.where(positions < 0, -1, counted).astype(jnp.int32)

def causal_conv(extended, ext_ids, conv_weight, conv_bias_v, length):
    kernel_len = conv_weight.shape[0]
    current = ext_ids[kernel_len - 1:kernel_len - 1 + length]
    summed = jnp.zeros((length, extended.shape[1]), jnp.float32) + conv_bias_v[None, :]
    for lag_rows in range(kernel_len):
        first_row = kernel_len - 1 - lag_rows
        shifted = extended[first_row:first_row + length]
        same_seq = (ext_ids[first_row:first_row + length] == current).astype(jnp.float32)
        summed = summed + conv_weight[kernel_len - 1 - lag_rows][None, :] * shifted * same_seq[:, None]
    return summed

def group_scan(ssm_state, group_in):
    head_block, dt_block, b_block, c_block, id_block, prior_id, rate_row = group_in
    row_count = head_block.shape[0]
    cumulative = jnp.cumsum(dt_block * rate_row[None, :], axis=0)
    order_ok = jnp.arange(row_count)[:, None] >= jnp.arange(row_count)[None, :]
    same_seq = (id_block[:, None] == id_block[None, :]) & order_ok
    differ = cumulative.T[:, :, None] - cumulative.T[:, None, :]
    decay_mat = jnp.exp(jnp.where(same_seq[None], differ, -jnp.inf))
    scores = jnp.dot(c_block, b_block.T, precision=highest)
    weights = scores[None] * decay_mat * dt_block.T[:, None, :]
    intra_out = jnp.einsum('hts,shp->thp', weights, head_block, precision=highest)
    carry_in = (id_block == prior_id).astype(jnp.float32)[:, None] * jnp.exp(cumulative)
    inter_out = jnp.einsum('tn,hpn->thp', c_block, ssm_state, precision=highest) * carry_in[:, :, None]
    tail_same = (id_block == id_block[row_count - 1])[:, None]
    tail_decay = jnp.exp(jnp.where(tail_same, cumulative[row_count - 1][None, :] - cumulative, -jnp.inf)) * dt_block
    new_state = ssm_state * carry_in[row_count - 1][:, None, None] + jnp.einsum('sh,shp,sn->hpn', tail_decay, head_block, b_block, precision=highest)
    return (new_state, intra_out + inter_out)

def ssd_parts(head_input, step_size, neg_rate, b_all, c_all, token_ids, prior_id):
    length, head_count, head_dim = head_input.shape
    group_count = length // GROUP
    group_ids = token_ids.reshape(group_count, GROUP)
    priors = jnp.concatenate([jnp.full((1,), -1, jnp.int32), group_ids[:group_count - 1, GROUP - 1]]).astype(jnp.int32)
    rates = jnp.broadcast_to(neg_rate[None, :], (group_count, head_count))
    zero_state = jnp.zeros((head_count, head_dim, b_all.shape[1]), jnp.float32)
    blocks = (head_input.reshape(group_count, GROUP, head_count, head_dim), step_size.reshape(group_count, GROUP, head_count), b_all.reshape(group_count, GROUP, b_all.shape[1]), c_all.reshape(group_count, GROUP, c_all.shape[1]), group_ids, priors, rates)
    final_state, outputs = lax.scan(jax.checkpoint(group_scan), zero_state, blocks)
    cumulative = jnp.cumsum(step_size * neg_rate[None, :], axis=0)
    carry_in = (token_ids == prior_id).astype(jnp.float32)[:, None] * jnp.exp(cumulative)
    return (outputs.reshape(length, head_count, head_dim), final_state, carry_in)

def mixer_layer(hidden, ext_ids, params):
    pre_gain, w_z, w_x, w_bc, w_dt, conv_x, conv_bc, conv_bias_x, conv_bias_bc, dt_bias, a_log, d_skip, inner_gain, w_out = params
    length = hidden.shape[0]
    normed = low(hidden * lax.rsqrt(lax.optimization_barrier(jnp.mean(hidden * hidden, axis=1, keepdims=True)) + epsilon) * pre_gain[None, :])
    gate_pre = low_back(jnp.dot(normed, w_z, precision=highest))
    x_pre = low_back(jnp.dot(normed, w_x, precision=highest))
    bc_pre = low_back(jnp.dot(normed, w_bc, precision=highest))
    dt_pre = low_back(jnp.dot(normed, w_dt, precision=highest))
    pre_conv = jnp.concatenate([x_pre, bc_pre], axis=1)
    extended = jnp.concatenate([jnp.zeros((CONV - 1, pre_conv.shape[1]), jnp.float32), pre_conv], axis=0)
    conv_weight = jnp.concatenate([conv_x, conv_bc], axis=1)
    conv_bias_v = jnp.concatenate([conv_bias_x, conv_bias_bc])
    active = silu_act(causal_conv(extended, ext_ids, conv_weight, conv_bias_v, length))
    head_input = active[:, :INNER].reshape(length, HEADS, HEADDIM)
    b_all = active[:, INNER:INNER + STATE]
    c_all = active[:, INNER + STATE:]
    step_size = jax.nn.softplus(dt_pre + dt_bias[None, :])
    neg_rate = -jnp.exp(a_log)
    token_ids = ext_ids[CONV - 1:]
    scanned, final_unused, carry_unused = ssd_parts(head_input, step_size, neg_rate, b_all, c_all, token_ids, jnp.int32(-1))
    mixed_out = scanned + d_skip[None, :, None] * head_input
    gated_out = mixed_out.reshape(length, INNER) * silu_act(gate_pre)
    normed_inner = low(gated_out * lax.rsqrt(lax.optimization_barrier(jnp.mean(gated_out * gated_out, axis=1, keepdims=True)) + epsilon) * inner_gain[None, :])
    return hidden + jnp.dot(normed_inner, w_out, precision=highest)

def reference(tokens, seq_lengths, cotangent, pre_gain, w_z, w_x, w_bc, w_dt, conv_x, conv_bc, conv_bias_x, conv_bias_bc, dt_bias, a_log, d_skip, inner_gain, w_out):
    positions = jnp.arange(MB_TOK + CONV - 1, dtype=jnp.int32) - (CONV - 1)
    ext_ids_all = [sequence_ids(seq_lengths[micro_index], positions) for micro_index in range(MICRO)]
    weight_list = tuple((item.astype(jnp.float32) for item in (pre_gain, w_z, w_x, w_bc, w_dt, conv_x, conv_bc, conv_bias_x, conv_bias_bc, dt_bias, a_log, d_skip, inner_gain, w_out)))

    def forward(tokens_f, probe, stacked):
        first_params = tuple((item[0] for item in stacked))
        second_params = tuple((item[1] for item in stacked))
        first_outs = []
        second_outs = []
        for micro_index in range(MICRO):
            first_out = mixer_layer(tokens_f[micro_index], ext_ids_all[micro_index], first_params)
            handed = low_back(low(first_out) + probe[micro_index])
            first_outs.append(handed)
            second_outs.append(mixer_layer(handed, ext_ids_all[micro_index], second_params))
        return (jnp.stack(first_outs), jnp.stack(second_outs))
    tokens_f = tokens.astype(jnp.float32)
    probe = jnp.zeros((MICRO, MB_TOK, D), jnp.float32)
    primals, pull_back = jax.vjp(forward, tokens_f, probe, weight_list)
    grad_tokens, grad_probe, grad_weights = pull_back((jnp.zeros_like(primals[0]), cotangent.astype(jnp.float32)))
    section_outputs = jnp.stack([primals[0], primals[1]]).astype(jnp.bfloat16)
    input_grads = jnp.stack([grad_tokens, grad_probe]).astype(jnp.bfloat16)
    return (section_outputs, input_grads, grad_weights[0], grad_weights[1], grad_weights[2], grad_weights[3], grad_weights[4], grad_weights[5], grad_weights[6], grad_weights[7], grad_weights[8], grad_weights[9], grad_weights[10], grad_weights[11], grad_weights[12], grad_weights[13])
```

```python
import functools
import types

import jax
import jax.numpy as jnp
from jax import lax
from jax.experimental import pallas as pl
from jax.experimental.pallas import tpu as pltpu
from jax.sharding import PartitionSpec as P

f32, bf16 = jnp.float32, jnp.bfloat16
EPS = 1e-05
CONV = 4
HD = 64
MESH = pl.DeviceIdType.MESH
RB = 64


def nn(a, b):
    return lax.dot_general(a, b, (((1,), (0,)), ((), ())), preferred_element_type=f32)


def nt(a, b):
    return lax.dot_general(a, b, (((1,), (1,)), ((), ())), preferred_element_type=f32)


def tn(a, b):
    return lax.dot_general(a, b, (((0,), (0,)), ((), ())), preferred_element_type=f32)


def iota(shape, axis):
    return lax.broadcasted_iota(jnp.int32, shape, axis)


def ones_where(condition, dtype=bf16):
    return jnp.where(condition, 1.0, 0.0).astype(dtype)


def sigmoid(v):
    return 1.0 / (1.0 + jnp.exp(-v))


def parts3(x):
    high = x.astype(bf16).astype(f32)
    rest = x - high
    middle = rest.astype(bf16).astype(f32)
    return [high, middle, rest - middle]


def columns_of(rows_list):
    parts = [p for x in rows_list for p in parts3(x)]
    length = rows_list[0].shape[1]
    parts.append(jnp.zeros((128 - 8 * len(parts), length), f32))
    return jnp.concatenate(parts, axis=0).T.astype(bf16)


def pick(which, width, row_of_lane):
    r, lane = iota((128, width), 0), iota((128, width), 1)
    mine = (r >= 24 * which) & (r < 24 * which + 24)
    return ones_where(mine & ((r & 7) == row_of_lane(lane)))


def over(total, block, body):
    def step(i, carry):
        body(pl.ds(pl.multiple_of(i * block, block), block), i)
        return carry

    lax.fori_loop(0, total // block, step, 0)


class Op:
    def __init__(self, k, send, recv, sent, received, when_send=None, when_recv=None):
        self.send, self.recv = k.send_sems.at[send], k.recv_sems.at[recv]
        self.sent, self.received = sent, received
        self.when_send, self.when_recv = when_send, when_recv

    def to(self, src, dst, **device):
        pltpu.make_async_remote_copy(
            src_ref=src,
            dst_ref=dst,
            send_sem=self.send,
            recv_sem=self.recv,
            device_id=device,
            device_id_type=MESH,
        ).start()

    def arrived(self):
        def wait():
            pltpu.make_async_copy(self.received, self.received, self.recv).wait()

        wait() if self.when_recv is None else pl.when(self.when_recv)(wait)

    def left(self):
        def wait():
            pltpu.make_async_copy(self.sent, self.sent, self.send).wait()

        wait() if self.when_send is None else pl.when(self.when_send)(wait)


def scratch_of(T, D, NC, S, TP, DP):
    TB = T // TP
    G2 = 2 * S
    v = pltpu.VMEM
    return dict(
        hb=v((2, T, D), bf16),
        n2=v((2, 2 * T, D), bf16),
        go2=v((2, 2 * T, D), bf16),
        wz=v((2, D, NC), bf16),
        wx=v((2, D, NC), bf16),
        wbc=v((2, D, G2), bf16),
        wdt=v((2, 128, D), bf16),
        wout=v((2, NC, D), bf16),
        pk=v((2, 16, D), f32),
        pkown=v((16, D), f32),
        cmask=v((3, T + 8, G2), f32),
        madd=v((T, T), f32),
        pmask=v((T, NC), f32),
        tmask=v((T, NC), f32),
        tri=v((T, T), bf16),
        xe=v((2, T + 8, NC), f32),
        be=v((2, T + 8, G2), f32),
        gate=v((2, T, NC), f32),
        va=v((2, T, NC), f32),
        vb=v((2, T, G2), f32),
        X=v((2, T, NC), f32),
        Bm=v((2, T, S), bf16),
        Cm=v((2, T, S), bf16),
        xt=v((2, T, NC), bf16),
        xtail=v((2, T, NC), bf16),
        blk=v((3 * T, NC), bf16),
        M=v((2, 3, T, T), f32),
        G=v((2, T, T), f32),
        Wc=v((2, T, 3 * T), bf16),
        ccs=v((T, 3 * T), f32),
        dte=v((2, T, NC), f32),
        cex=v((T, NC), f32),
        ee=v((2, T, NC), f32),
        tl=v((2, T, NC), f32),
        stp=v((2, 8, T), f32),
        arow=v((2, 8, T), f32),
        sgd=v((2, 8, T), f32),
        yv=v((T, NC), f32),
        yin=v((2, T, NC), f32),
        mx=v((2, T, NC), f32),
        gd=v((2, T, NC), f32),
        gg=v((2, T, NC), bf16),
        sq=v((T, NC), bf16),
        sq2=v((T, NC), bf16),
        gni=v((T, NC), f32),
        s0=v((2, S, NC), f32),
        stS=v((4, S + 16, 256), bf16),
        stR=v((4, DP - 1, S + 16, 256), bf16),
        arS=v((2, 8, T), f32),
        arR=v((2, TP - 1, 8, T), f32),
        us=v((4, T, D), bf16),
        ur=v((4, TP - 1, TB, D), bf16),
        own=v((4, TB, D), bf16),
        u0=v((TB, D), f32),
        rex=v((2, T, NC), f32),
        kex=v((T, NC), f32),
        crossS=v((TB, 256), f32),
        cross=v((T, 256), f32),
        gm=v((T, NC), f32),
        eg=v((T, NC), bf16),
        gz2=v((2, 2 * T, NC), bf16),
        gx2=v((2, 2 * T, NC), bf16),
        ni2=v((2, 2 * T, NC), bf16),
        gdt2=v((2, 8, 2 * T), f32),
        dxt=v((T, NC), f32),
        dW=v((3, T, T), f32),
        Pb=v((3, T, T), bf16),
        dG=v((T, T), bf16),
        bes=v((T, NC), f32),
        qs=v((T, NC), bf16),
        gis=v((T, NC), bf16),
        dds=v((T, NC), bf16),
        dbc=v((T, G2), f32),
        ux=v((2, T + 8, NC), f32),
        ub=v((2, T + 8, G2), f32),
        gbp=v((2, T, G2), bf16),
        gbr=v((2, TP - 1, TB, G2), bf16),
        gbo=v((2, TB, G2), bf16),
        gb2=v((2, 2 * T, G2), bf16),
        nT=v((D, 2 * T), bf16),
        dzS=v((2, D, NC), bf16),
        dzR=v((2, DP - 1, D // DP, NC), bf16),
        dzO=v((2, D // DP, NC), bf16),
        dxS=v((2, D, NC), bf16),
        dxR=v((2, DP - 1, D // DP, NC), bf16),
        dxO=v((2, D // DP, NC), bf16),
        doS=v((2, NC, D), bf16),
        doR=v((2, DP - 1, NC // DP, D), bf16),
        doO=v((2, NC // DP, D), bf16),
        dbS=v((2, D // TP, G2), bf16),
        dbR=v((2, DP - 1, D // TP, G2), bf16),
        dbO=v((2, D // TP, G2), bf16),
        dtS=v((2, 8, D), f32),
        dtR=v((2, DP - 1, 8, D), f32),
        gpS=v((2, 8, 384), f32),
        gpR=v((2, TP - 1, 8, 384), f32),
        fpS=v((2, 24, 384), f32),
        fpR=v((2, 2 * DP - 1, 24, 384), f32),
        w_sems=pltpu.SemaphoreType.DMA((6, 2)),
        l_sems=pltpu.SemaphoreType.DMA((24,)),
        send_sems=pltpu.SemaphoreType.DMA((96,)),
        recv_sems=pltpu.SemaphoreType.DMA((96,)),
    )


INPUTS = (
    "i_tokens",
    "i_cot",
    "i_wz",
    "i_wx",
    "i_wbc",
    "i_wdt",
    "i_wout",
    "i_pre",
    "i_cx",
    "i_cbc",
    "i_bx",
    "i_bbc",
    "i_gain",
    "i_seq",
    "i_dtb",
    "i_alog",
    "i_dsk",
)
OUTPUTS = ("o_sec", "o_ing", "o_wz", "o_wx", "o_wbc", "o_wout", "o_dt", "o_pack")


def kernel(geo, names, *refs):
    k = types.SimpleNamespace(**dict(zip(names, refs)))
    T, D, NC, S, TP, DP = geo
    TB, G2, INNER = T // TP, 2 * S, NC * TP
    c, d, t = lax.axis_index("pipe"), lax.axis_index("dp"), lax.axis_index("tensor")
    other = 1 - c
    mine = pl.ds(pl.multiple_of(t * TB, TB), TB)
    ids = iter(range(96))
    pending = []

    def op(sent, received, when_send=None, when_recv=None):
        i = next(ids)
        made = Op(k, i, i, sent, received, when_send, when_recv)
        pending.append(made)
        return made

    def local(src, dst, i):
        return pltpu.make_async_copy(src, dst, k.l_sems.at[i])

    def peers(body, first=1):
        def step(j, carry):
            body(j, lax.rem(t + j, TP))
            return carry

        lax.fori_loop(first, TP, step, 0)

    in_tokens = local(k.i_tokens.at[c], k.hb.at[0], 0)
    in_tokens.start()
    weights = [("wx", 0), ("wbc", 1), ("wdt", 2), ("wz", 3), ("wout", 4)]

    def held(name):
        ref = getattr(k, name)
        return ref.at[c, 0:16] if name == "wdt" else ref.at[c]

    for name, i in weights:
        pltpu.make_async_copy(getattr(k, "i_" + name).at[0], held(name), k.w_sems.at[i, c]).start()
    in_cot = local(k.i_cot.at[c], k.go2.at[1, 0:T], 1)
    in_cot.start()
    in_cot_other = local(k.i_cot.at[other], k.go2.at[1, T : 2 * T], 2)
    in_cot_other.start()

    pk = k.pkown
    pk[...] = jnp.zeros_like(pk)
    pk[0:1, :] = k.i_pre[...]
    pk[1:5, 0:NC] = k.i_cx[0]
    pk[1:5, 256 : 256 + G2] = k.i_cbc[0]
    pk[5:6, 0:NC] = k.i_bx[...]
    pk[5:6, 256 : 256 + G2] = k.i_bbc[...]
    pk[6:7, 0:NC] = k.i_gain[...]
    head = iota((1, NC), 1) // HD
    skip = jnp.zeros((1, NC), f32)
    for h in range(3):
        pk[8 + h : 9 + h, 0:T] = jnp.full((1, T), k.i_dtb[0, h], f32)
        pk[8 + h : 9 + h, T : 2 * T] = jnp.full((1, T), k.i_alog[0, h], f32)
        skip = jnp.where(head == h, k.i_dsk[0, h], skip)
    pk[7:8, 0:NC] = skip
    pltpu.make_async_copy(k.pkown, k.pk.at[c], k.w_sems.at[5, c]).start()

    barrier = pltpu.get_barrier_semaphore()

    def greet(**device):
        pl.semaphore_signal(barrier, inc=1, device_id=device, device_id_type=MESH)

    peers(lambda j, to: greet(tensor=to))
    peers(lambda j, to: greet(pipe=other, tensor=to), 0)
    for j in range(1, DP):
        greet(dp=lax.rem(d + j, DP))
        greet(pipe=other, dp=lax.rem(d + j, DP))
    pl.semaphore_wait(barrier, 2 * TP - 1 + 2 * (DP - 1))

    w_sent = []

    def give(src, dst, i):
        send = k.send_sems.at[next(ids)]
        copy = pltpu.make_async_remote_copy(
            src_ref=src,
            dst_ref=dst,
            send_sem=send,
            recv_sem=k.w_sems.at[i, c],
            device_id={"pipe": other},
            device_id_type=MESH,
        )
        copy.start()
        w_sent.append(copy)

    give(k.pkown, k.pk.at[c], 5)
    for name, i in weights:
        give(getattr(k, "i_" + name).at[0], held(name), i)

    def have(name, i, l):
        ref = getattr(k, name)
        ref = ref.at[l, 0:16] if name == "wdt" else ref.at[l]
        pltpu.make_async_copy(ref, ref, k.w_sems.at[i, l]).wait()

    first_end = k.i_seq[c, 0]
    second_end = first_end + k.i_seq[c, 1]

    def seq_id(p):
        counted = jnp.where(p >= first_end, 1, 0) + jnp.where(p >= second_end, 1, 0)
        return jnp.where(p < 0, -1, counted)

    start = d * T
    for lag in range(1, CONV):
        p = start + iota((T + 8, G2), 0)
        k.cmask[lag - 1] = ones_where(seq_id(p) == seq_id(p - lag), f32)
    p_row, p_col = start + iota((T, T), 0), start + iota((T, T), 1)
    k.madd[...] = jnp.where((seq_id(p_row) == seq_id(p_col)) & (p_row >= p_col), 0.0, -1e30)
    k.tri[...] = ones_where(p_row <= p_col)
    p_row = start + iota((T, NC), 0)
    id_row = seq_id(p_row)
    k.pmask[...] = ones_where(id_row == seq_id(p_row * 0 + (start - 1)), f32)
    k.tmask[...] = ones_where(id_row == seq_id(p_row * 0 + (start + T - 1)), f32)
    for l in range(2):
        k.wdt[l, 16:128, :] = jnp.zeros((112, D), bf16)

    def running(x, backward=False):
        p = jnp.concatenate(parts3(x) + [jnp.zeros_like(x)], axis=0).astype(bf16)
        y = nt(p, k.tri[...]) if backward else nn(p, k.tri[...])
        return y[0:8] + y[8:16] + y[16:24]

    def heads_of(lane):
        return lane // HD

    per_head = ones_where(iota((8, NC), 0) == iota((8, NC), 1) // HD)

    def joined(slot, have_k):
        total, through = jnp.zeros((S, NC), f32), jnp.ones((1, NC), f32)
        for j in range(1, DP):
            part = k.stR[slot, j - 1, 0:S, 0:NC].astype(f32)
            decay = k.stR[slot, j - 1, S : S + 16, 0:NC].astype(f32)[0:1]
            total = total + (through * have_k(j)) * part
            through = through * decay
        return total

    def scatter(slot):
        made = op(k.ur.at[slot], k.ur.at[slot])

        def body(j, to):
            rows = pl.ds(pl.multiple_of(to * TB, TB), TB)
            made.to(k.us.at[slot, rows], k.ur.at[slot, j - 1], tensor=to)

        peers(body)
        return made

    def summed(made, slot):
        made.arrived()
        total = k.us[slot, mine, :].astype(f32)
        for j in range(TP - 1):
            total = total + k.ur[slot, j].astype(f32)
        return total

    def forward(l):
        have("pk", 5, l)

        def norm(r, i):
            h = k.hb[l, r, :].astype(f32)
            scale = lax.rsqrt(jnp.mean(h * h, axis=1, keepdims=True) + EPS)
            k.n2[l, r, :] = (h * scale * k.pk[l, 0:1, :]).astype(bf16)

        over(T, 32, norm)
        send_n = op(k.n2.at[l, 0:T], k.n2.at[l, T : 2 * T], c != l, c == l)
        pl.when(c != l)(
            lambda: send_n.to(k.n2.at[l, 0:T], k.n2.at[l, T : 2 * T], pipe=other)
        )
        have("wx", 0, l)
        k.xe[l, 8 : 8 + T, :] = nn(k.n2[l, 0:T, :], k.wx[l])
        have("wbc", 1, l)
        k.be[l, 8 : 8 + T, :] = nn(k.n2[l, 0:T, :], k.wbc[l])
        halo_x = op(k.xe.at[l, T : T + 8], k.xe.at[l, 0:8])
        halo_b = op(k.be.at[l, T : T + 8], k.be.at[l, 0:8])
        after = lax.rem(d + 1, DP)
        halo_x.to(k.xe.at[l, T : T + 8], k.xe.at[l, 0:8], dp=after)
        halo_b.to(k.be.at[l, T : T + 8], k.be.at[l, 0:8], dp=after)
        have("wdt", 2, l)
        dtp = nt(k.wdt[l, 0:16, :], k.n2[l, 0:T, :])[0:8] + k.pk[l, 8:16, 0:T]
        step = jnp.maximum(dtp, 0.0) + jnp.log1p(jnp.exp(-jnp.abs(dtp)))
        a = -jnp.exp(k.pk[l, 8:16, T : 2 * T]) * step
        run = running(a)
        k.stp[l], k.arow[l], k.sgd[l] = step, a, sigmoid(dtp)
        have("wz", 3, l)
        k.gate[l] = nn(k.n2[l, 0:T, :], k.wz[l])
        cols = columns_of([run, step])
        k.cex[...] = nn(cols, pick(0, NC, heads_of))
        k.dte[l] = nn(cols, pick(1, NC, heads_of))
        k.ccs[...] = nn(cols, pick(0, 3 * T, lambda lane: lane // T))

        def decays(r, i):
            here = k.cex[r, :]
            k.ee[l, r, :] = jnp.exp(here) * k.pmask[r, :]
            k.tl[l, r, :] = jnp.exp(k.cex[T - 1 : T, :] - here) * k.tmask[r, :]

        over(T, RB, decays)
        halo_x.arrived()
        halo_b.arrived()

        def conv(r, i):
            near = pl.ds(pl.multiple_of(i * RB, RB), RB + 8)
            for ext, lane, width in ((k.xe, 0, NC), (k.be, 256, G2)):
                block = ext[l, near, :]
                lanes = slice(lane, lane + width)
                v = k.pk[l, 5:6, lanes] + k.pk[l, 4:5, lanes] * block[8:]
                for lag in range(1, CONV):
                    moved = block[8 - lag : RB + 8 - lag] * k.cmask[lag - 1, r, 0:width]
                    v = v + k.pk[l, 4 - lag : 5 - lag, lanes] * moved
                act = v * sigmoid(v)
                if lane == 0:
                    k.va[l, r, :] = v
                    k.X[l, r, :] = act
                    xt = act * k.dte[l, r, :]
                    k.xt[l, r, :] = xt.astype(bf16)
                    k.xtail[l, r, :] = (xt * k.tl[l, r, :]).astype(bf16)
                    for h in range(3):
                        at = pl.ds(pl.multiple_of(h * T + i * RB, RB), RB)
                        k.blk[at, :] = jnp.where(head == h, xt, 0.0).astype(bf16)
                else:
                    k.vb[l, r, :] = v
                    k.Bm[l, r, :] = act[:, 0:S].astype(bf16)
                    k.Cm[l, r, :] = act[:, S:G2].astype(bf16)

        over(T, RB, conv)
        k.stS[l, 0:S, 0:NC] = tn(k.Bm[l], k.xtail[l]).astype(bf16)
        k.stS[l, S : S + 16, 0:NC] = jnp.broadcast_to(k.ee[l, T - 1 : T, :], (16, NC)).astype(bf16)
        states = op(k.stR.at[l], k.stR.at[l])
        for j in range(1, DP):
            states.to(k.stS.at[l], k.stR.at[l, j - 1], dp=lax.rem(d + j, DP))
        k.G[l] = nt(k.Cm[l], k.Bm[l])

        def mixing(r, i):
            for h in range(3):
                lanes = slice(h * T, h * T + T)
                m = jnp.exp(k.ccs[r, lanes] - run[h : h + 1, :] + k.madd[r, :])
                k.M[l, h, r, :] = m
                k.Wc[l, r, lanes] = (k.G[l, r, :] * m).astype(bf16)

        over(T, 32, mixing)
        k.yv[...] = nn(k.Wc[l], k.blk[...])
        if l == 1:
            have("wout", 4, l)
            k.gni[...] = nt(k.go2[1, 0:T, :], k.wout[1])
        states.arrived()
        k.s0[l] = joined(l, lambda j: jnp.where(d >= j, 1.0, 0.0))
        k.yin[l] = nn(k.Cm[l], k.s0[l].astype(bf16)) * k.ee[l]

        def gating(r, i):
            z = k.gate[l, r, :]
            mixed = k.yv[r, :] + k.yin[l, r, :] + k.pk[l, 7:8, 0:NC] * k.X[l, r, :]
            gated = mixed * z * sigmoid(z)
            k.mx[l, r, :] = mixed
            k.gd[l, r, :] = gated
            scaled = gated * k.pk[l, 6:7, 0:NC]
            k.gg[l, r, :] = scaled.astype(bf16)
            k.sq[r, :] = (gated * gated).astype(bf16)
            if l == 1:
                k.sq2[r, :] = (scaled * k.gni[r, :]).astype(bf16)

        over(T, RB, gating)
        row = iota((8, NC), 0)
        sums = nt(ones_where(row == 0), k.sq[...])
        if l == 1:
            sums = sums + nt(ones_where(row == 1), k.sq2[...])
        k.arS[l] = sums
        small = op(k.arR.at[l], k.arR.at[l])
        peers(lambda j, to: small.to(k.arS.at[l], k.arR.at[l, j - 1], tensor=to))
        if l == 0:
            have("wout", 4, l)
        for j in range(D // 256):
            lanes = slice(256 * j, 256 * j + 256)
            k.us[l, :, lanes] = nn(k.gg[l], k.wout[l, :, lanes]).astype(bf16)
        made = scatter(l)
        small.arrived()
        total = k.arS[l]
        for j in range(TP - 1):
            total = total + k.arR[l, j]
        r = lax.rsqrt(total[0:1] / INNER + EPS)
        factor = r * r * r * (total[1:2] / INNER)
        cols = columns_of([jnp.concatenate([r, factor, jnp.zeros((6, T), f32)], axis=0)])
        k.rex[l] = nn(cols, pick(0, NC, lambda lane: 0 * lane))
        if l == 1:
            k.kex[...] = nn(cols, pick(0, NC, lambda lane: 0 * lane + 1))
        return made, send_n

    def section_rows(l, made):
        total = summed(made, l)
        if l == 0:
            k.u0[...] = total
        out = k.hb[l, mine, :].astype(f32) + k.rex[l, mine, 0:1] * total
        k.own[l] = out.astype(bf16)

    def spread_out(slot, out, l):
        near = op(out.at[0, 0, 0 : T - TB], out.at[0, 0, 0 : T - TB], c == l, c == l)
        far = op(out.at[0, 0, 0:T], out.at[0, 0, 0:T], c != l, c == l)
        dst = out.at[0, c, mine]
        keep = local(k.own.at[slot], dst, 8 + slot)

        @pl.when(c == l)
        def _():
            peers(lambda j, to: near.to(k.own.at[slot], dst, tensor=to))
            keep.start()

        @pl.when(c != l)
        def _():
            peers(lambda j, to: far.to(k.own.at[slot], dst, pipe=other, tensor=to), 0)

        return near, far, lambda: pl.when(c == l)(keep.wait)

    def gather_in(slot, buffer):
        made = op(buffer.at[0 : T - TB], buffer.at[0 : T - TB])
        dst = buffer.at[mine]
        peers(lambda j, to: made.to(k.own.at[slot], dst, tensor=to))
        dst[...] = k.own[slot]
        return made

    def hand_out(src, out, l, i):
        far = op(src, out.at[0, 0], c != l, c == l)
        keep = local(src, out.at[0, c], i)

        @pl.when(c == l)
        def _():
            keep.start()

        @pl.when(c != l)
        def _():
            far.to(src, out.at[0, c], pipe=other)

        return far, lambda: pl.when(c == l)(keep.wait)

    def backward(l):
        if l == 0:
            k.gni[...] = nt(k.go2[0, 0:T, :], k.wout[0])

        def gates(r, i, sums):
            z = k.gate[l, r, :]
            s = sigmoid(z)
            gn, gated, rx = k.gni[r, :], k.gd[l, r, :], k.rex[l, r, :]
            if l == 1:
                factor = k.kex[r, :]
            else:
                factor = rx * rx * rx * (k.cross[r, 0:NC] / INNER)
            gain = k.pk[l, 6:7, 0:NC]
            g = rx * (gn * gain) - gated * factor
            gm = g * z * s
            gz = g * k.mx[l, r, :] * s * (1.0 + z * (1.0 - s))
            k.gm[r, :] = gm
            k.gz2[l, r, :] = gz.astype(bf16)
            k.eg[r, :] = (gm * k.ee[l, r, :]).astype(bf16)
            k.ni2[l, r, :] = (gated * gain * rx).astype(bf16)
            for h in range(3):
                at = pl.ds(pl.multiple_of(h * T + i * RB, RB), RB)
                k.blk[at, :] = jnp.where(head == h, gm, 0.0).astype(bf16)
            by_gain = jnp.sum(gn * gated * rx, axis=0, keepdims=True)
            by_skip = jnp.sum(gm * k.X[l, r, :], axis=0, keepdims=True)
            return sums[0] + by_gain, sums[1] + by_skip

        zero = jnp.zeros((1, NC), f32)
        by_gain, by_skip = lax.fori_loop(
            0,
            T // RB,
            lambda i, s: gates(pl.ds(pl.multiple_of(i * RB, RB), RB), i, s),
            (zero, zero),
        )
        k.fpS[l] = jnp.zeros((24, 384), f32)
        k.fpS[l, 13:14, 0:NC] = by_gain
        k.fpS[l, 14:15, 0:NC] = by_skip
        k.stS[2 + l, 0:S, 0:NC] = tn(k.Cm[l], k.eg[...]).astype(bf16)
        k.stS[2 + l, S : S + 16, 0:NC] = k.stS[l, S : S + 16, 0:NC]
        states = op(k.stR.at[2 + l], k.stR.at[2 + l])
        for j in range(1, DP):
            states.to(k.stS.at[2 + l], k.stR.at[2 + l, j - 1], dp=lax.rem(d + DP - j, DP))
        dxt = jnp.zeros((T, NC), f32)
        for h in range(3):
            part = k.blk[h * T : h * T + T, :]
            dxt = dxt + tn(k.Wc[l, :, h * T : h * T + T], part)
            k.dW[h] = nt(part, k.xt[l])
        k.dxt[...] = dxt

        def pairs(r, i):
            g_sum = jnp.zeros((32, T), f32)
            for h in range(3):
                w = k.dW[h, r, :] * k.M[l, h, r, :]
                g_sum = g_sum + w
                k.Pb[h, r, :] = (w * k.G[l, r, :]).astype(bf16)
            k.dG[r, :] = g_sum.astype(bf16)

        over(T, 32, pairs)
        flow = jnp.zeros((8, T), f32)
        for h in range(3):
            one = ones_where(iota((8, T), 0) == h)
            flow = flow + nt(one, k.Pb[h]) - nn(one, k.Pb[h])
        states.arrived()
        after = joined(2 + l, lambda j: jnp.where(d + j < DP, 1.0, 0.0))
        through = jnp.sum(after * k.s0[l], axis=0, keepdims=True) * k.ee[l, T - 1 : T, :]
        constant = jnp.sum(per_head.astype(f32) * through, axis=1, keepdims=True)
        after = after.astype(bf16)
        k.bes[...] = nn(k.Bm[l], after)
        k.dbc[:, 0:S] = tn(k.dG[...], k.Cm[l]) + nt(k.xtail[l], after)
        k.dbc[:, S:G2] = nn(k.dG[...], k.Bm[l]) + nt(k.eg[...], k.s0[l].astype(bf16))

        def inputs(r, i):
            x, gm, dte = k.X[l, r, :], k.gm[r, :], k.dte[l, r, :]
            tail = k.tl[l, r, :] * k.bes[r, :]
            dx = k.dxt[r, :] + tail
            k.qs[r, :] = (x * dte * tail).astype(bf16)
            k.gis[r, :] = (gm * k.yin[l, r, :]).astype(bf16)
            k.dds[r, :] = (dx * x).astype(bf16)
            v = k.va[l, r, :]
            s = sigmoid(v)
            k.ux[l, r, :] = (dte * dx + k.pk[l, 7:8, 0:NC] * gm) * (s * (1.0 + v * (1.0 - s)))
            v = k.vb[l, r, :]
            s = sigmoid(v)
            k.ub[l, r, :] = k.dbc[r, :] * (s * (1.0 + v * (1.0 - s)))

        over(T, RB, inputs)
        halo_x = op(k.ux.at[l, 0:8], k.ux.at[l, T : T + 8])
        halo_b = op(k.ub.at[l, 0:8], k.ub.at[l, T : T + 8])
        before = lax.rem(d + DP - 1, DP)
        halo_x.to(k.ux.at[l, 0:8], k.ux.at[l, T : T + 8], dp=before)
        halo_b.to(k.ub.at[l, 0:8], k.ub.at[l, T : T + 8], dp=before)
        q, inter = nt(per_head, k.qs[...]), nt(per_head, k.gis[...])
        direct = nt(per_head, k.dds[...])
        da = running(flow + inter, True) + (running(q) - q) + constant
        a_log = k.pk[l, 8:16, T : 2 * T]
        gdt = (direct - jnp.exp(a_log) * da) * k.sgd[l]
        k.gdt2[l, :, 0:T] = gdt
        k.fpS[l, 16:24, 0:128] = jnp.broadcast_to(jnp.sum(gdt, axis=1, keepdims=True), (8, 128))
        by_a = jnp.sum(k.arow[l] * da, axis=1, keepdims=True)
        k.fpS[l, 16:24, 128:256] = jnp.broadcast_to(by_a, (8, 128))
        halo_x.arrived()
        halo_b.arrived()

        def conv_back(u, ext, lane, width, dst):
            lanes = slice(lane, lane + width)

            def step(i, sums):
                near = pl.ds(pl.multiple_of(i * RB, RB), RB + 8)
                r = pl.ds(pl.multiple_of(i * RB, RB), RB)
                ublock, before = u[l, near, :], ext[l, near, :]
                g = k.pk[l, 4:5, lanes] * ublock[0:RB]
                here = ublock[0:RB]
                out = [
                    sums[0] + jnp.sum(here * before[8:], axis=0, keepdims=True),
                ]
                for lag in range(1, CONV):
                    masked = ublock * k.cmask[lag - 1, near, 0:width]
                    g = g + k.pk[l, 4 - lag : 5 - lag, lanes] * masked[lag : RB + lag]
                    moved = before[8 - lag : RB + 8 - lag]
                    out.append(
                        sums[lag] + jnp.sum(masked[0:RB] * moved, axis=0, keepdims=True)
                    )
                out.append(sums[CONV] + jnp.sum(here, axis=0, keepdims=True))
                dst[l, r, :] = g.astype(bf16)
                return tuple(out)

            zero = jnp.zeros((1, width), f32)
            return lax.fori_loop(0, T // RB, step, (zero,) * (CONV + 1))

        by_bc = conv_back(k.ub, k.be, 256, G2, k.gbp)
        bc = op(k.gbr.at[l], k.gbr.at[l])

        def give_bc(j, to):
            rows = pl.ds(pl.multiple_of(to * TB, TB), TB)
            bc.to(k.gbp.at[l, rows], k.gbr.at[l, j - 1], tensor=to)

        peers(give_bc)
        by_x = conv_back(k.ux, k.xe, 0, NC, k.gx2)
        k.gpS[l] = jnp.zeros((8, 384), f32)
        for lag in range(CONV):
            k.fpS[l, 8 + 3 - lag : 9 + 3 - lag, 0:NC] = by_x[lag]
            k.gpS[l, 4 + 3 - lag : 5 + 3 - lag, 0:G2] = by_bc[lag]
        k.fpS[l, 12:13, 0:NC] = by_x[CONV]
        k.gpS[l, 4:5, G2 : G2 + 128] = by_bc[CONV][:, 0:128]
        k.gpS[l, 5:6, G2 : G2 + 128] = by_bc[CONV][:, 128:256]
        gdt_cols = jnp.concatenate([gdt, jnp.zeros((120, T), f32)], axis=0).T.astype(bf16)
        for j in range(D // 256):
            at = slice(256 * j, 256 * j + 256)
            part = nt(k.gz2[l, 0:T, :], k.wz[l, at, :]) + nt(k.gx2[l, 0:T, :], k.wx[l, at, :])
            part = part + nt(k.gbp[l], k.wbc[l, at, :]) + nn(gdt_cols, k.wdt[l, :, at])
            k.us[2 + l, :, at] = part.astype(bf16)
        return scatter(2 + l), bc

    def input_rows(l, made):
        gn = summed(made, 2 + l)
        h = k.hb[l, mine, :].astype(f32)
        scale = lax.rsqrt(jnp.mean(h * h, axis=1, keepdims=True) + EPS)
        weighted = gn * k.pk[l, 0:1, :]
        inner = jnp.sum(weighted * h, axis=1, keepdims=True)
        gh = scale * weighted - h * (scale * scale * scale * (1.0 / D) * inner)
        low = (k.go2[l, mine, :].astype(f32) + gh).astype(bf16)
        k.own[2 + l] = low
        by_pre = jnp.sum(gn * h * scale, axis=0, keepdims=True)
        for j in range(4):
            k.gpS[l, j : j + 1, :] = by_pre[:, 384 * j : 384 * j + 384]
        if l == 1:
            sums = jnp.sum(low.astype(f32) * k.u0[...], axis=1, keepdims=True)
            k.crossS[...] = jnp.broadcast_to(sums, (TB, 256))

    def operands(l):
        pairs = [(k.gz2.at[l, 0:T], k.gz2.at[l, T : 2 * T])]
        pairs += [(k.gx2.at[l, 0:T], k.gx2.at[l, T : 2 * T])]
        pairs += [(k.ni2.at[l, 0:T], k.ni2.at[l, T : 2 * T])]
        pairs += [(k.gdt2.at[l, :, 0:T], k.gdt2.at[l, :, T : 2 * T])]
        ops = [op(a, b, c != l, c == l) for a, b in pairs]

        @pl.when(c != l)
        def _():
            for made, (a, b) in zip(ops, pairs):
                made.to(a, b, pipe=other)

        return ops

    def bc_total(l, bc):
        bc.arrived()
        total = k.gbp[l, mine, :].astype(f32)
        for j in range(TP - 1):
            total = total + k.gbr[l, j].astype(f32)
        k.gbo[l] = total.astype(bf16)
        near = op(k.gb2.at[l, 0 : T - TB], k.gb2.at[l, 0 : T - TB], c == l, c == l)
        far = op(k.gb2.at[l, 0:T], k.gb2.at[l, 0:T], c != l, c == l)

        @pl.when(c == l)
        def _():
            peers(lambda j, to: near.to(k.gbo.at[l], k.gb2.at[l, mine], tensor=to))
            k.gb2[l, mine, :] = k.gbo[l]

        @pl.when(c != l)
        def _():
            there = pl.ds(pl.multiple_of(T + t * TB, TB), TB)
            peers(
                lambda j, to: far.to(k.gbo.at[l], k.gb2.at[l, there], pipe=other, tensor=to),
                0,
            )

        return near, far

    def ring(l, name, axis_rows):
        sent, recv = getattr(k, name + "S"), getattr(k, name + "R")
        made = op(recv.at[l], recv.at[l], c == l, c == l)

        def start():
            for j in range(1, DP):
                to = lax.rem(d + j, DP)
                rows = pl.ds(pl.multiple_of(to * axis_rows, axis_rows), axis_rows)
                made.to(sent.at[l, rows], recv.at[l, j - 1], dp=to)

        return made, start

    def ring_end(l, name, made, out, axis_rows):
        sent, recv, own = (getattr(k, name + x) for x in "SRO")
        rows = pl.ds(pl.multiple_of(d * axis_rows, axis_rows), axis_rows)
        total_rows = axis_rows * (DP - 1)
        spread = op(out.at[0, 0:total_rows], out.at[0, 0:total_rows], c == l, c == l)

        def finish():
            made.arrived()
            total = sent[l, rows, :].astype(f32)
            for j in range(DP - 1):
                total = total + recv[l, j].astype(f32)
            own[l] = total.astype(bf16)
            for j in range(1, DP):
                spread.to(own.at[l], out.at[0, rows], dp=lax.rem(d + j, DP))

        return spread, finish, (own.at[l], out.at[0, rows])

    def weight_grads(l, n_op, factor_ops, bc_ops, go_op):
        dz, start_z = ring(l, "dz", D // DP)
        dx, start_x = ring(l, "dx", D // DP)
        do, start_o = ring(l, "do", NC // DP)
        dt_made = op(k.dtR.at[l], k.dtR.at[l], c == l, c == l)
        db_made = op(k.dbR.at[l], k.dbR.at[l], c == l, c == l)

        @pl.when(c == l)
        def _():
            pltpu.make_async_copy(n_op.received, n_op.received, n_op.recv).wait()
            for made in factor_ops:
                pltpu.make_async_copy(made.received, made.received, made.recv).wait()
            if go_op is not None:
                pltpu.make_async_copy(go_op.received, go_op.received, go_op.recv).wait()
            for j in range(D // 128):
                at = slice(128 * j, 128 * j + 128)
                k.nT[at, :] = k.n2[l, :, at].T
            k.dxS[l] = nn(k.nT[...], k.gx2[l]).astype(bf16)
            start_x()
            k.dzS[l] = nn(k.nT[...], k.gz2[l]).astype(bf16)
            start_z()
            for j in range(D // 256):
                at = slice(256 * j, 256 * j + 256)
                k.doS[l, :, at] = tn(k.ni2[l], k.go2[l, :, at]).astype(bf16)
            start_o()
            steps = jnp.concatenate([k.gdt2[l], jnp.zeros((8, 2 * T), f32)], axis=0).astype(bf16)
            k.dtS[l] = nn(steps, k.n2[l])[0:8]
            for j in range(1, DP):
                dt_made.to(k.dtS.at[l], k.dtR.at[l, j - 1], dp=lax.rem(d + j, DP))
            for made in bc_ops:
                pltpu.make_async_copy(made.received, made.received, made.recv).wait()
            part = pl.ds(pl.multiple_of(t * (D // TP), D // TP), D // TP)
            k.dbS[l] = nn(k.nT[part, :], k.gb2[l]).astype(bf16)
            for j in range(1, DP):
                db_made.to(k.dbS.at[l], k.dbR.at[l, j - 1], dp=lax.rem(d + j, DP))

        return dz, dx, do, dt_made, db_made

    def weight_ends(l, made):
        dz, dx, do, dt_made, db_made = made
        ends = [
            ring_end(l, "dx", dx, k.o_wx, D // DP),
            ring_end(l, "dz", dz, k.o_wz, D // DP),
            ring_end(l, "do", do, k.o_wout, NC // DP),
        ]
        slab = D // TP
        rows = pl.ds(pl.multiple_of(t * slab, slab), slab)
        count = slab * (TP - 1)
        spread = op(k.o_wbc.at[0, 0:count], k.o_wbc.at[0, 0:count], c == l, c == l)

        @pl.when(c == l)
        def _():
            copies = []
            for i, (_, finish, (src, dst)) in enumerate(ends):
                finish()
                copies.append(local(src, dst, 12 + i))
                copies[-1].start()
            db_made.arrived()
            total = k.dbS[l].astype(f32)
            for j in range(DP - 1):
                total = total + k.dbR[l, j].astype(f32)
            k.dbO[l] = total.astype(bf16)
            peers(lambda j, to: spread.to(k.dbO.at[l], k.o_wbc.at[0, rows], tensor=to))
            copies.append(local(k.dbO.at[l], k.o_wbc.at[0, rows], 15))
            copies[-1].start()
            dt_made.arrived()
            total = k.dtS[l]
            for j in range(DP - 1):
                total = total + k.dtR[l, j]
            k.o_dt[...] = total
            for copy in copies:
                copy.wait()

        return [e[0] for e in ends] + [spread]

    def small_start(l):
        made = op(k.gpR.at[l], k.gpR.at[l])
        peers(lambda j, to: made.to(k.gpS.at[l], k.gpR.at[l, j - 1], tensor=to))
        return made

    def small_middle(l, made):
        made.arrived()
        total = k.gpS[l]
        for j in range(TP - 1):
            total = total + k.gpR[l, j]
        k.fpS[l, 0:8, :] = total
        near = op(k.fpR.at[l, 0 : DP - 1], k.fpR.at[l, 0 : DP - 1], c == l, c == l)
        far = op(k.fpR.at[l, DP - 1 :], k.fpR.at[l, DP - 1 :], c != l, c == l)

        @pl.when(c == l)
        def _():
            for j in range(1, DP):
                near.to(k.fpS.at[l], k.fpR.at[l, j - 1], dp=lax.rem(d + j, DP))

        @pl.when(c != l)
        def _():
            for j in range(DP):
                far.to(k.fpS.at[l], k.fpR.at[l, DP - 1 + j], pipe=other, dp=lax.rem(d + j, DP))

        return near, far

    def small_end(l, made):
        for m in made:
            m.arrived()

        @pl.when(c == l)
        def _():
            total = k.fpS[l]
            for j in range(2 * DP - 1):
                total = total + k.fpR[l, j]
            k.o_pack[...] = total

    in_tokens.wait()
    made, n_op0 = forward(0)
    section_rows(0, made)
    gather = gather_in(0, k.hb.at[1])
    gather.arrived()
    sec0, sec0_keep = hand_out(k.hb.at[1], k.o_sec, 0, 3)
    in_cot.wait()
    in_cot_other.wait()
    made1, n_op1 = forward(1)
    made2, bc1 = backward(1)
    factors1 = operands(1)
    section_rows(1, made1)
    sec1 = spread_out(1, k.o_sec, 1)
    input_rows(1, made2)
    gather = gather_in(3, k.go2.at[0, 0:T])
    cross = op(k.cross.at[0 : T - TB], k.cross.at[0 : T - TB])
    peers(lambda j, to: cross.to(k.crossS, k.cross.at[mine], tensor=to))
    k.cross[mine, :] = k.crossS[...]
    small1 = small_start(1)
    bc_ops1 = bc_total(1, bc1)
    gather.arrived()
    cross.arrived()
    ing1, ing1_keep = hand_out(k.go2.at[0, 0:T], k.o_ing, 1, 4)
    go_op = op(k.go2.at[0, 0:T], k.go2.at[0, T : 2 * T], c != 0, c == 0)
    pl.when(c != 0)(
        lambda: go_op.to(k.go2.at[0, 0:T], k.go2.at[0, T : 2 * T], pipe=other)
    )
    grads1 = weight_grads(1, n_op1, factors1, bc_ops1, None)
    made3, bc0 = backward(0)
    factors0 = operands(0)
    bc_ops0 = bc_total(0, bc0)
    grads0 = weight_grads(0, n_op0, factors0, bc_ops0, go_op)
    packs1 = small_middle(1, small1)
    spreads = weight_ends(1, grads1)
    input_rows(0, made3)
    ing0 = spread_out(2, k.o_ing, 0)
    small0 = small_start(0)
    spreads += weight_ends(0, grads0)
    packs0 = small_middle(0, small0)
    small_end(1, packs1)
    small_end(0, packs0)
    sec0.arrived()
    sec0_keep()
    ing1.arrived()
    ing1_keep()
    for near, far, keep in (sec1, ing0):
        near.arrived()
        far.arrived()
        keep()
    for spread in spreads:
        spread.arrived()
    for copy in w_sent:
        copy.wait_send()
    for made in pending:
        made.left()


def on_device(sizes, *args):
    (tokens, seq, cot, pre, wz, wx, wbc, wdt, cx, cbc, bx, bbc, dtb, alog, dsk, gain, wout) = args
    TP, DP = sizes
    _, T, D = tokens.shape
    NC, S = wx.shape[2], wbc.shape[2] // 2
    wdt = jnp.pad(jnp.swapaxes(wdt, 1, 2), ((0, 0), (0, 13), (0, 0)))
    scratch = scratch_of(T, D, NC, S, TP, DP)
    names = tuple(INPUTS) + tuple(OUTPUTS) + tuple(scratch)
    any_, vmem, smem = (pl.BlockSpec(memory_space=m) for m in (pl.ANY, pltpu.VMEM, pltpu.SMEM))
    made = pl.pallas_call(
        functools.partial(kernel, (T, D, NC, S, TP, DP), names),
        out_shape=(
            jax.ShapeDtypeStruct((1, 2, T, D), bf16),
            jax.ShapeDtypeStruct((1, 2, T, D), bf16),
            jax.ShapeDtypeStruct((1, D, NC), bf16),
            jax.ShapeDtypeStruct((1, D, NC), bf16),
            jax.ShapeDtypeStruct((1, D, 2 * S), bf16),
            jax.ShapeDtypeStruct((1, NC, D), bf16),
            jax.ShapeDtypeStruct((8, D), f32),
            jax.ShapeDtypeStruct((24, 384), f32),
        ),
        in_specs=[any_] * 7 + [vmem] * 6 + [smem] * 4,
        out_specs=(any_,) * 6 + (vmem,) * 2,
        scratch_shapes=list(scratch.values()),
        compiler_params=pltpu.CompilerParams(
            collective_id=0, has_side_effects=True, vmem_limit_bytes=60 * 1024 * 1024
        ),
    )(tokens, cot, wz, wx, wbc, wdt, wout, pre, cx, cbc, bx, bbc, gain, seq, dtb, alog, dsk)
    sec, ing, dwz, dwx, dwbc, dwout, ddt, pack = made
    heads = NC // HD
    by_skip = pack[14, 0:NC].reshape(1, heads, HD).sum(axis=2)
    return (
        sec,
        ing,
        pack[0:4].reshape(1, D),
        dwz.astype(f32),
        dwx.astype(f32),
        dwbc.astype(f32),
        ddt[0:heads].T[None],
        pack[8:12, 0:NC][None],
        pack[4:8, 0 : 2 * S][None],
        pack[12:13, 0:NC],
        pack[4:6, 256:384].reshape(1, 2 * S),
        pack[16 : 16 + heads, 0][None],
        pack[16 : 16 + heads, 128][None],
        by_skip,
        pack[13:14, 0:NC],
        dwout.astype(f32),
    )


def solution(mesh):
    in_specs = (
        P(None, "dp", None),
        P(),
        P(None, "dp", None),
        P("pipe", None),
        P("pipe", None, "tensor"),
        P("pipe", None, "tensor"),
        P("pipe", None, None),
        P("pipe", None, "tensor"),
        P("pipe", None, "tensor"),
        P("pipe", None, None),
        P("pipe", "tensor"),
        P("pipe", None),
        P("pipe", "tensor"),
        P("pipe", "tensor"),
        P("pipe", "tensor"),
        P("pipe", "tensor"),
        P("pipe", "tensor", None),
    )
    out_specs = (
        P("pipe", None, "dp", None),
        P("pipe", None, "dp", None),
        P("pipe", None),
        P("pipe", None, "tensor"),
        P("pipe", None, "tensor"),
        P("pipe", None, None),
        P("pipe", None, "tensor"),
        P("pipe", None, "tensor"),
        P("pipe", None, None),
        P("pipe", "tensor"),
        P("pipe", None),
        P("pipe", "tensor"),
        P("pipe", "tensor"),
        P("pipe", "tensor"),
        P("pipe", "tensor"),
        P("pipe", "tensor", None),
    )
    return jax.shard_map(
        functools.partial(on_device, (mesh.shape["tensor"], mesh.shape["dp"])),
        mesh=mesh,
        in_specs=in_specs,
        out_specs=out_specs,
        check_vma=False,
    )
```

```python
import functools
import types

import jax
import jax.numpy as jnp
from jax import lax
from jax.experimental import pallas as pl
from jax.experimental.pallas import tpu as pltpu
from jax.sharding import PartitionSpec as P

f32, bf16 = jnp.float32, jnp.bfloat16
EPS = 1e-05
CONV = 4
HD = 64
MESH = pl.DeviceIdType.MESH
RB = 64


def nn(a, b):
    return lax.dot_general(a, b, (((1,), (0,)), ((), ())), preferred_element_type=f32)


def nt(a, b):
    return lax.dot_general(a, b, (((1,), (1,)), ((), ())), preferred_element_type=f32)


def tn(a, b):
    return lax.dot_general(a, b, (((0,), (0,)), ((), ())), preferred_element_type=f32)


def iota(shape, axis):
    return lax.broadcasted_iota(jnp.int32, shape, axis)


def ones_where(condition, dtype=bf16):
    return jnp.where(condition, 1.0, 0.0).astype(dtype)


def sigmoid(v):
    return 1.0 / (1.0 + jnp.exp(-v))


def parts3(x):
    high = x.astype(bf16).astype(f32)
    rest = x - high
    middle = rest.astype(bf16).astype(f32)
    return [high, middle, rest - middle]


def columns_of(rows_list):
    parts = [p for x in rows_list for p in parts3(x)]
    length = rows_list[0].shape[1]
    parts.append(jnp.zeros((128 - 8 * len(parts), length), f32))
    return jnp.concatenate(parts, axis=0).T.astype(bf16)


def pick(which, width, row_of_lane):
    r, lane = iota((128, width), 0), iota((128, width), 1)
    mine = (r >= 24 * which) & (r < 24 * which + 24)
    return ones_where(mine & ((r & 7) == row_of_lane(lane)))


def over(total, block, body):
    def step(i, carry):
        body(pl.ds(pl.multiple_of(i * block, block), block), i)
        return carry

    lax.fori_loop(0, total // block, step, 0)


class Op:
    def __init__(self, k, send, recv, sent, received, when_send=None, when_recv=None):
        self.send, self.recv = k.send_sems.at[send], k.recv_sems.at[recv]
        self.sent, self.received = sent, received
        self.when_send, self.when_recv = when_send, when_recv

    def to(self, src, dst, **device):
        pltpu.make_async_remote_copy(
            src_ref=src,
            dst_ref=dst,
            send_sem=self.send,
            recv_sem=self.recv,
            device_id=device,
            device_id_type=MESH,
        ).start()

    def beside(self, received, when_recv):
        made = object.__new__(Op)
        made.recv, made.received, made.when_recv = self.recv, received, when_recv
        return made

    def take(self):
        pltpu.make_async_copy(self.received, self.received, self.recv).wait()

    def arrived(self):
        self.take() if self.when_recv is None else pl.when(self.when_recv)(self.take)

    def left(self):
        def wait():
            pltpu.make_async_copy(self.sent, self.sent, self.send).wait()

        wait() if self.when_send is None else pl.when(self.when_send)(wait)


def scratch_of(T, D, NC, S, TZ, TX, DP):
    TP = TZ * TX
    TB, H = T // TP, D // 2
    G2, slab = 2 * S, max(128, D // TP)
    v = pltpu.VMEM
    return dict(
        hb=v((2, TZ, TX, TB, D), bf16),
        n2=v((2, 2 * T, D), bf16),
        go2=v((2, 2, TZ, TX, TB, D), bf16),
        wz=v((2, NC, D), bf16),
        wx=v((2, NC, D), bf16),
        wbc=v((2, D, G2), bf16),
        wdt=v((2, 128, D), bf16),
        wout=v((2, NC, D), bf16),
        pk=v((2, 16, D), f32),
        pkown=v((16, D), f32),
        cmask=v((3, T + 8, G2), f32),
        madd=v((T, T), f32),
        pmask=v((T, NC), f32),
        tmask=v((T, NC), f32),
        tri=v((T, T), bf16),
        xe=v((2, T + 8, NC), f32),
        be=v((2, T + 8, G2), f32),
        gate=v((2, T, NC), f32),
        va=v((2, T, NC), f32),
        vb=v((2, T, G2), f32),
        X=v((2, T, NC), f32),
        Bm=v((2, T, S), bf16),
        Cm=v((2, T, S), bf16),
        xt=v((2, T, NC), bf16),
        xtail=v((2, T, NC), bf16),
        blk=v((3 * T, NC), bf16),
        M=v((2, 3, T, T), f32),
        G=v((2, T, T), f32),
        Wc=v((2, T, 3 * T), bf16),
        ccs=v((T, 3 * T), f32),
        dte=v((2, T, NC), f32),
        cex=v((T, NC), f32),
        ee=v((2, T, NC), f32),
        tl=v((2, T, NC), f32),
        arow=v((2, 8, T), f32),
        sgd=v((2, 8, T), f32),
        yv=v((T, NC), f32),
        yin=v((2, T, NC), f32),
        mx=v((2, T, NC), f32),
        gd=v((2, T, NC), f32),
        gg=v((2, T, NC), bf16),
        sq=v((T, NC), bf16),
        sq2=v((T, NC), bf16),
        gni=v((T, NC), f32),
        s0=v((2, NC, S), f32),
        eT=v((2, 8, S), f32),
        stS=v((4, NC + 16, S), bf16),
        stR=v((4, DP - 1, NC + 16, S), bf16),
        arS=v((2, 8, T // 2), f32),
        arR=v((2, TP - 1, 8, T // 2), f32),
        us=v((4, TZ, TX, TB, D), bf16),
        r1a=v((4, TZ - 1, TX, TB, H), bf16),
        r1b=v((4, TX - 1, TZ, TB, H), bf16),
        ma=v((4, TX, TB, H), bf16),
        mb=v((4, TZ, TB, H), bf16),
        r2a=v((4, TX - 1, TB, H), bf16),
        r2b=v((4, TZ - 1, TB, H), bf16),
        own=v((2, TB, D), bf16),
        u0=v((TB, D), f32),
        rex=v((2, T, NC), f32),
        kex=v((T, NC), f32),
        crossS=v((TB, 128), f32),
        cross=v((T, 128), f32),
        gm=v((T, NC), f32),
        eg=v((T, NC), bf16),
        gz2=v((2, 2 * T, NC), bf16),
        gx2=v((2, 2 * T, NC), bf16),
        ni2=v((2, 2 * T, NC), bf16),
        gdt2=v((2, 8, 2 * T), f32),
        dxt=v((T, NC), f32),
        dW=v((3, T, T), f32),
        Pb=v((3, T, T), bf16),
        dG=v((T, T), bf16),
        bes=v((T, NC), f32),
        qs=v((T, NC), bf16),
        gis=v((T, NC), bf16),
        dds=v((T, NC), bf16),
        dbc=v((T, G2), f32),
        ux=v((2, T + 8, NC), f32),
        ub=v((2, T + 8, G2), f32),
        gbp=v((2, T, G2), bf16),
        gbr=v((2, TP - 1, TB, G2), bf16),
        gbo=v((2, TB, G2), bf16),
        gb2=v((2, 2 * T, G2), bf16),
        dzS=v((2, NC, D), bf16),
        dzR=v((2, DP - 1, NC // DP, D), bf16),
        dzO=v((2, NC // DP, D), bf16),
        dxS=v((2, NC, D), bf16),
        dxR=v((2, DP - 1, NC // DP, D), bf16),
        dxO=v((2, NC // DP, D), bf16),
        doS=v((2, NC, D), bf16),
        doR=v((2, DP - 1, NC // DP, D), bf16),
        doO=v((2, NC // DP, D), bf16),
        dbS=v((2, slab, G2), bf16),
        dbR=v((2, DP - 1, slab, G2), bf16),
        dbO=v((2, slab, G2), bf16),
        dtS=v((2, 8, D), f32),
        dtR=v((2, DP - 1, 8, D), f32),
        gpS=v((2, 8, 384), f32),
        gpR=v((2, TP - 1, 8, 384), f32),
        fpS=v((2, 24, 384), f32),
        fpR=v((2, 2 * DP - 1, 24, 384), f32),
        w_sems=pltpu.SemaphoreType.DMA((6, 2)),
        l_sems=pltpu.SemaphoreType.DMA((24,)),
        send_sems=pltpu.SemaphoreType.DMA((160,)),
        recv_sems=pltpu.SemaphoreType.DMA((160,)),
    )


INPUTS = (
    "i_tokens",
    "i_cot",
    "i_wz",
    "i_wx",
    "i_wbc",
    "i_wdt",
    "i_wout",
    "i_pre",
    "i_cx",
    "i_cbc",
    "i_bx",
    "i_bbc",
    "i_gain",
    "i_seq",
    "i_dtb",
    "i_alog",
    "i_dsk",
)
OUTPUTS = ("o_sec", "o_ing", "o_wz", "o_wx", "o_wbc", "o_wout", "o_dt", "o_pack")


def kernel(geo, names, *refs):
    k = types.SimpleNamespace(**dict(zip(names, refs)))
    T, D, NC, S, TZ, TX, DP = geo
    TP = TZ * TX
    TB, G2, INNER, H = T // TP, 2 * S, NC * TP, D // 2
    FIRST, SECOND = slice(0, H), slice(H, D)
    slab = max(128, D // TP)
    slabs = D // slab
    c, d, t = lax.axis_index("pipe"), lax.axis_index("dp"), lax.axis_index("tensor")
    other = 1 - c
    tz, tx = t // TX, lax.rem(t, TX)
    mine = pl.ds(pl.multiple_of(t * TB, TB), TB)
    ids = iter(range(160))
    pending = []

    def op(sent, received, when_send=None, when_recv=None):
        i = next(ids)
        made = Op(k, i, i, sent, received, when_send, when_recv)
        pending.append(made)
        return made

    def local(src, dst, i):
        return pltpu.make_async_copy(src, dst, k.l_sems.at[i])

    def peers(body, first=1):
        def step(j, carry):
            body(j, lax.rem(t + j, TP))
            return carry

        lax.fori_loop(first, TP, step, 0)

    barrier = pltpu.get_barrier_semaphore()

    def greet(**device):
        pl.semaphore_signal(barrier, inc=1, device_id=device, device_id_type=MESH)

    peers(lambda j, to: greet(pipe=other, tensor=to), 0)
    peers(lambda j, to: greet(tensor=to))
    for j in range(1, DP):
        greet(dp=lax.rem(d + j, DP))
        greet(pipe=other, dp=lax.rem(d + j, DP))

    in_tokens = local(k.i_tokens.at[c], k.hb.at[0], 0)
    in_tokens.start()
    weights = [("wx", 0), ("wbc", 1), ("wdt", 2), ("wz", 3), ("wout", 4)]

    def held(name):
        ref = getattr(k, name)
        return ref.at[c, 0:16] if name == "wdt" else ref.at[c]

    for name, i in weights:
        pltpu.make_async_copy(getattr(k, "i_" + name).at[0], held(name), k.w_sems.at[i, c]).start()
    in_cot = local(k.i_cot.at[c], k.go2.at[1, 0], 1)
    in_cot.start()
    in_cot_other = local(k.i_cot.at[other], k.go2.at[1, 1], 2)
    in_cot_other.start()

    pk = k.pkown
    pk[...] = jnp.zeros_like(pk)
    pk[0:1, :] = k.i_pre[...]
    pk[1:5, 0:NC] = k.i_cx[0]
    pk[1:5, 256 : 256 + G2] = k.i_cbc[0]
    pk[5:6, 0:NC] = k.i_bx[...]
    pk[5:6, 256 : 256 + G2] = k.i_bbc[...]
    pk[6:7, 0:NC] = k.i_gain[...]
    head = iota((1, NC), 1) // HD
    skip = jnp.zeros((1, NC), f32)
    for h in range(3):
        pk[8 + h : 9 + h, 0:T] = jnp.full((1, T), k.i_dtb[0, h], f32)
        pk[8 + h : 9 + h, T : 2 * T] = jnp.full((1, T), k.i_alog[0, h], f32)
        skip = jnp.where(head == h, k.i_dsk[0, h], skip)
    pk[7:8, 0:NC] = skip
    pltpu.make_async_copy(k.pkown, k.pk.at[c], k.w_sems.at[5, c]).start()

    first_end = k.i_seq[c, 0]
    second_end = first_end + k.i_seq[c, 1]

    def seq_id(p):
        counted = jnp.where(p >= first_end, 1, 0) + jnp.where(p >= second_end, 1, 0)
        return jnp.where(p < 0, -1, counted)

    start = d * T
    for lag in range(1, CONV):
        p = start + iota((T + 8, G2), 0)
        k.cmask[lag - 1] = ones_where(seq_id(p) == seq_id(p - lag), f32)
    p_row, p_col = start + iota((T, T), 0), start + iota((T, T), 1)
    k.madd[...] = jnp.where((seq_id(p_row) == seq_id(p_col)) & (p_row >= p_col), 0.0, -1e30)
    k.tri[...] = ones_where(p_row <= p_col)
    p_row = start + iota((T, NC), 0)
    id_row = seq_id(p_row)
    k.pmask[...] = ones_where(id_row == seq_id(p_row * 0 + (start - 1)), f32)
    k.tmask[...] = ones_where(id_row == seq_id(p_row * 0 + (start + T - 1)), f32)
    for l in range(2):
        k.wdt[l, 16:128, :] = jnp.zeros((112, D), bf16)

    pl.semaphore_wait(barrier, 2 * TP - 1 + 2 * (DP - 1))

    w_sent = []

    def give(src, dst, i):
        send = k.send_sems.at[next(ids)]
        copy = pltpu.make_async_remote_copy(
            src_ref=src,
            dst_ref=dst,
            send_sem=send,
            recv_sem=k.w_sems.at[i, c],
            device_id={"pipe": other},
            device_id_type=MESH,
        )
        copy.start()
        w_sent.append(copy)

    give(k.pkown, k.pk.at[c], 5)
    for name, i in weights:
        give(getattr(k, "i_" + name).at[0], held(name), i)

    def have(name, i, l):
        ref = getattr(k, name)
        ref = ref.at[l, 0:16] if name == "wdt" else ref.at[l]
        pltpu.make_async_copy(ref, ref, k.w_sems.at[i, l]).wait()

    def running(x, backward=False):
        p = jnp.concatenate(parts3(x) + [jnp.zeros_like(x)], axis=0).astype(bf16)
        y = nt(p, k.tri[...]) if backward else nn(p, k.tri[...])
        return y[0:8] + y[8:16] + y[16:24]

    def heads_of(lane):
        return lane // HD

    per_head = ones_where(iota((8, NC), 0) == iota((8, NC), 1) // HD)

    def states_to(slot, backward):
        ops = []
        for j in range(1, DP):
            src, dst = k.stS.at[slot], k.stR.at[slot, j - 1]
            up, down = d + j < DP, d >= j
            made = op(src, dst, down if backward else up, up if backward else down)
            to = lax.rem(d + (DP - j if backward else j), DP)
            pl.when(down if backward else up)(lambda: made.to(src, dst, dp=to))
            ops.append(made)
        return ops

    def joined(slot, backward):
        blocks = [jnp.zeros((HD, S), f32)] * 3
        through = jnp.ones((8, S), f32)
        for j in range(1, DP):
            there = d + j < DP if backward else d >= j
            part = k.stR[slot, j - 1, 0:NC, :].astype(f32)
            for h in range(3):
                term = through[h : h + 1] * part[HD * h : HD * h + HD]
                blocks[h] = blocks[h] + jnp.where(there, term, 0.0)
            decay = k.stR[slot, j - 1, NC : NC + 16, :].astype(f32)[0:8]
            through = through * jnp.where(there, decay, 0.0)
        return jnp.concatenate(blocks, axis=0)

    def z_peers(body):
        for j in sorted(range(1, TZ), key=lambda j: min(j, TZ - j)):
            q = lax.rem(tz + j, TZ)
            body(j, q, q * TX + tx)

    def x_peers(body):
        for j in sorted(range(1, TX), key=lambda j: min(j, TX - j)):
            p = lax.rem(tx + j, TX)
            body(j, p, tz * TX + p)

    def scatter(slot):
        a1, b1 = (op(r.at[slot], r.at[slot]) for r in (k.r1a, k.r1b))
        z_peers(lambda j, q, to: a1.to(k.us.at[slot, q, :, :, FIRST], k.r1a.at[slot, j - 1], tensor=to))
        x_peers(lambda j, p, to: b1.to(k.us.at[slot, :, p, :, SECOND], k.r1b.at[slot, j - 1], tensor=to))
        return a1, b1

    def scatter_on(slot, made):
        a2, b2 = (op(r.at[slot], r.at[slot]) for r in (k.r2a, k.r2b))
        made[0].arrived()
        total = k.us[slot, tz, :, :, FIRST].astype(f32)
        for j in range(TZ - 1):
            total = total + k.r1a[slot, j].astype(f32)
        k.ma[slot] = total.astype(bf16)
        x_peers(lambda j, p, to: a2.to(k.ma.at[slot, p], k.r2a.at[slot, j - 1], tensor=to))
        made[1].arrived()
        total = k.us[slot, :, tx, :, SECOND].astype(f32)
        for j in range(TX - 1):
            total = total + k.r1b[slot, j].astype(f32)
        k.mb[slot] = total.astype(bf16)
        z_peers(lambda j, q, to: b2.to(k.mb.at[slot, q], k.r2b.at[slot, j - 1], tensor=to))
        return a2, b2

    def summed(made, slot):
        made[0].arrived()
        first = k.ma[slot, tx].astype(f32)
        for j in range(TX - 1):
            first = first + k.r2a[slot, j].astype(f32)
        made[1].arrived()
        second = k.mb[slot, tz].astype(f32)
        for j in range(TZ - 1):
            second = second + k.r2b[slot, j].astype(f32)
        return jnp.concatenate([first, second], axis=1)

    def gather(buffer, rows):
        buffer[tz, tx] = rows
        done = buffer.at[0, 0 : TX - 1, :, FIRST], buffer.at[0 : TZ - 1, 0, :, SECOND]
        a1, b1 = (op(r, r) for r in done)
        first, second = buffer.at[tz, tx, :, FIRST], buffer.at[tz, tx, :, SECOND]
        x_peers(lambda j, p, to: a1.to(first, first, tensor=to))
        z_peers(lambda j, q, to: b1.to(second, second, tensor=to))
        return a1, b1

    def gather_on(buffer, made):
        done = buffer.at[0 : TZ - 1, :, :, FIRST], buffer.at[:, 0 : TX - 1, :, SECOND]
        a2, b2 = (op(r, r) for r in done)
        first, second = buffer.at[tz, :, :, FIRST], buffer.at[:, tx, :, SECOND]
        made[0].arrived()
        z_peers(lambda j, q, to: a2.to(first, first, tensor=to))
        made[1].arrived()
        x_peers(lambda j, p, to: b2.to(second, second, tensor=to))
        return a2, b2

    def both(made):
        for m in made:
            m.arrived()

    def forward(l):
        have("pk", 5, l)

        def norm(r, i):
            pair = pl.ds(lax.rem(i, TX // 2) * 2, 2)
            h = k.hb[l, i // (TX // 2), pair].reshape(2 * TB, D).astype(f32)
            scale = lax.rsqrt(jnp.mean(h * h, axis=1, keepdims=True) + EPS)
            k.n2[l, r, :] = (h * scale * k.pk[l, 0:1, :]).astype(bf16)

        over(T, 2 * TB, norm)
        send_n = op(k.n2.at[l, 0:T], k.n2.at[l, T : 2 * T], c != l, c == l)
        pl.when(c != l)(
            lambda: send_n.to(k.n2.at[l, 0:T], k.n2.at[l, T : 2 * T], pipe=other)
        )
        have("wx", 0, l)
        k.xe[l, 8 : 8 + T, :] = nt(k.n2[l, 0:T, :], k.wx[l])
        have("wbc", 1, l)
        k.be[l, 8 : 8 + T, :] = nn(k.n2[l, 0:T, :], k.wbc[l])
        halo_x = op(k.xe.at[l, T : T + 8], k.xe.at[l, 0:8])
        halo_b = op(k.be.at[l, T : T + 8], k.be.at[l, 0:8])
        after = lax.rem(d + 1, DP)
        halo_x.to(k.xe.at[l, T : T + 8], k.xe.at[l, 0:8], dp=after)
        halo_b.to(k.be.at[l, T : T + 8], k.be.at[l, 0:8], dp=after)
        have("wdt", 2, l)
        dtp = nt(k.wdt[l, 0:16, :], k.n2[l, 0:T, :])[0:8] + k.pk[l, 8:16, 0:T]
        step = jnp.maximum(dtp, 0.0) + jnp.log1p(jnp.exp(-jnp.abs(dtp)))
        a = -jnp.exp(k.pk[l, 8:16, T : 2 * T]) * step
        run = running(a)
        k.arow[l], k.sgd[l] = a, sigmoid(dtp)
        k.eT[l] = jnp.broadcast_to(jnp.exp(run[:, T - 1 : T]) * k.pmask[T - 1 : T, 0:1], (8, S))
        cols = columns_of([run, step])
        k.cex[...] = nn(cols, pick(0, NC, heads_of))
        k.dte[l] = nn(cols, pick(1, NC, heads_of))
        k.ccs[...] = nn(cols, pick(0, 3 * T, lambda lane: lane // T))

        def decays(r, i):
            here = k.cex[r, :]
            k.ee[l, r, :] = jnp.exp(here) * k.pmask[r, :]
            k.tl[l, r, :] = jnp.exp(k.cex[T - 1 : T, :] - here) * k.tmask[r, :]

        over(T, RB, decays)
        halo_x.arrived()
        halo_b.arrived()

        def conv(r, i):
            near = pl.ds(pl.multiple_of(i * RB, RB), RB + 8)
            for ext, lane, width in ((k.xe, 0, NC), (k.be, 256, G2)):
                block = ext[l, near, :]
                lanes = slice(lane, lane + width)
                v = k.pk[l, 5:6, lanes] + k.pk[l, 4:5, lanes] * block[8:]
                for lag in range(1, CONV):
                    moved = block[8 - lag : RB + 8 - lag] * k.cmask[lag - 1, r, 0:width]
                    v = v + k.pk[l, 4 - lag : 5 - lag, lanes] * moved
                act = v * sigmoid(v)
                if lane == 0:
                    k.va[l, r, :] = v
                    k.X[l, r, :] = act
                    xt = act * k.dte[l, r, :]
                    k.xt[l, r, :] = xt.astype(bf16)
                    k.xtail[l, r, :] = (xt * k.tl[l, r, :]).astype(bf16)
                    for h in range(3):
                        at = pl.ds(pl.multiple_of(h * T + i * RB, RB), RB)
                        k.blk[at, :] = jnp.where(head == h, xt, 0.0).astype(bf16)
                else:
                    k.vb[l, r, :] = v
                    k.Bm[l, r, :] = act[:, 0:S].astype(bf16)
                    k.Cm[l, r, :] = act[:, S:G2].astype(bf16)

        over(T, RB, conv)
        k.stS[l, 0:NC, :] = tn(k.xtail[l], k.Bm[l]).astype(bf16)
        ends = jnp.concatenate([k.eT[l], jnp.zeros((8, S), f32)], axis=0)
        k.stS[l, NC : NC + 16, :] = ends.astype(bf16)
        states = states_to(l, False)
        have("wz", 3, l)
        k.gate[l] = nt(k.n2[l, 0:T, :], k.wz[l])
        k.G[l] = nt(k.Cm[l], k.Bm[l])

        def mixing(r, i):
            for h in range(3):
                lanes = slice(h * T, h * T + T)
                m = jnp.exp(k.ccs[r, lanes] - run[h : h + 1, :] + k.madd[r, :])
                k.M[l, h, r, :] = m
                k.Wc[l, r, lanes] = (k.G[l, r, :] * m).astype(bf16)

        over(T, 32, mixing)
        k.yv[...] = nn(k.Wc[l], k.blk[...])
        if l == 1:
            have("wout", 4, l)
            k.gni[...] = nt(k.go2[1, 0].reshape(T, D), k.wout[1])
        both(states)
        k.s0[l] = joined(l, False)
        k.yin[l] = nt(k.Cm[l], k.s0[l].astype(bf16)) * k.ee[l]

        def gating(r, i):
            z = k.gate[l, r, :]
            mixed = k.yv[r, :] + k.yin[l, r, :] + k.pk[l, 7:8, 0:NC] * k.X[l, r, :]
            gated = mixed * z * sigmoid(z)
            k.mx[l, r, :] = mixed
            k.gd[l, r, :] = gated
            scaled = gated * k.pk[l, 6:7, 0:NC]
            k.gg[l, r, :] = scaled.astype(bf16)
            k.sq[r, :] = (gated * gated).astype(bf16)
            if l == 1:
                k.sq2[r, :] = (scaled * k.gni[r, :]).astype(bf16)

        over(T, RB, gating)
        row = iota((8, NC), 0)
        sums = nt(ones_where(row == 0), k.sq[...])
        if l == 1:
            sums = sums + nt(ones_where(row == 1), k.sq2[...])
        halves = [sums[0:1, 0 : T // 2], sums[0:1, T // 2 :], sums[1:2, 0 : T // 2], sums[1:2, T // 2 :]]
        k.arS[l] = jnp.concatenate(halves + [jnp.zeros((4, T // 2), f32)], axis=0)
        small = op(k.arR.at[l], k.arR.at[l])
        peers(lambda j, to: small.to(k.arS.at[l], k.arR.at[l, j - 1], tensor=to))
        if l == 0:
            have("wout", 4, l)
        for j in range(D // 256):
            lanes = slice(256 * j, 256 * j + 256)
            part = nn(k.gg[l], k.wout[l, :, lanes]).astype(bf16)
            k.us[l, :, :, :, lanes] = part.reshape(TZ, TX, TB, 256)
        made = scatter(l)
        small.arrived()
        total = k.arS[l]
        for j in range(TP - 1):
            total = total + k.arR[l, j]
        squares = jnp.concatenate([total[0:1], total[1:2]], axis=1)
        r = lax.rsqrt(squares / INNER + EPS)
        factor = r * r * r * (jnp.concatenate([total[2:3], total[3:4]], axis=1) / INNER)
        cols = columns_of([jnp.concatenate([r, factor, jnp.zeros((6, T), f32)], axis=0)])
        k.rex[l] = nn(cols, pick(0, NC, lambda lane: 0 * lane))
        if l == 1:
            k.kex[...] = nn(cols, pick(0, NC, lambda lane: 0 * lane + 1))
        return made, send_n

    def section_rows(l, made):
        total = summed(made, l)
        if l == 0:
            k.u0[...] = total
        return (k.hb[l, tz, tx].astype(f32) + k.rex[l, mine, 0:1] * total).astype(bf16)

    def spread(src, out, l, i):
        near_a, near_b = out.at[0, 0, 0, 0 : TX - 1, :, FIRST], out.at[0, 0, 0 : TZ - 1, 0, :, SECOND]
        far_a, far_b = out.at[0, 0, 0, 0:TX, :, FIRST], out.at[0, 0, 0:TZ, 0, :, SECOND]
        na, nb = (op(x, x, c == l, c == l) for x in (near_a, near_b))
        fa, fb = (op(x, x, c != l, c == l) for x in (far_a, far_b))
        dst = out.at[0, c, tz, tx]
        first, second = dst.at[:, FIRST], dst.at[:, SECOND]
        keep = local(src, dst, i)

        @pl.when(c == l)
        def _():
            x_peers(lambda j, p, to: na.to(src.at[:, FIRST], first, tensor=to))
            z_peers(lambda j, q, to: nb.to(src.at[:, SECOND], second, tensor=to))
            keep.start()

        @pl.when(c != l)
        def _():
            for p in range(TX):
                fa.to(src.at[:, FIRST], first, pipe=other, tensor=tz * TX + p)
            for q in range(TZ):
                fb.to(src.at[:, SECOND], second, pipe=other, tensor=q * TX + tx)

        return na, nb, fa, fb, keep

    def spread_on(out, l, made):
        na, nb, fa, fb, keep = made
        done_a, done_b = out.at[0, 0, 0 : TZ - 1, :, :, FIRST], out.at[0, 0, :, 0 : TX - 1, :, SECOND]
        ops = [op(x, x, c == l, c == l) for x in (done_a, done_b, done_a, done_b)]
        mine_a, mine_b = out.at[0, c, tz, :, :, FIRST], out.at[0, c, :, tx, :, SECOND]
        that_a, that_b = out.at[0, other, tz, :, :, FIRST], out.at[0, other, :, tx, :, SECOND]

        @pl.when(c == l)
        def _():
            keep.wait()
            na.take()
            z_peers(lambda j, q, to: ops[0].to(mine_a, mine_a, tensor=to))
            nb.take()
            x_peers(lambda j, p, to: ops[1].to(mine_b, mine_b, tensor=to))
            fa.take()
            z_peers(lambda j, q, to: ops[2].to(that_a, that_a, tensor=to))
            fb.take()
            x_peers(lambda j, p, to: ops[3].to(that_b, that_b, tensor=to))

        return ops

    def hand_out(src, out, l, i):
        far = op(src, out.at[0, 0], c != l, c == l)
        keep = local(src, out.at[0, c], i)

        @pl.when(c == l)
        def _():
            keep.start()

        @pl.when(c != l)
        def _():
            far.to(src, out.at[0, c], pipe=other)

        return far, lambda: pl.when(c == l)(keep.wait)

    def backward(l, meanwhile):
        if l == 0:
            k.gni[...] = nt(k.go2[0, 0].reshape(T, D), k.wout[0])

        def gates(r, i, sums):
            z = k.gate[l, r, :]
            s = sigmoid(z)
            gn, gated, rx = k.gni[r, :], k.gd[l, r, :], k.rex[l, r, :]
            if l == 1:
                factor = k.kex[r, :]
            else:
                factor = rx * rx * rx * (k.cross[r, 0:1] / INNER)
            gain = k.pk[l, 6:7, 0:NC]
            g = rx * (gn * gain) - gated * factor
            gm = g * z * s
            gz = g * k.mx[l, r, :] * s * (1.0 + z * (1.0 - s))
            k.gm[r, :] = gm
            k.gz2[l, r, :] = gz.astype(bf16)
            k.eg[r, :] = (gm * k.ee[l, r, :]).astype(bf16)
            k.ni2[l, r, :] = (gated * gain * rx).astype(bf16)
            for h in range(3):
                at = pl.ds(pl.multiple_of(h * T + i * RB, RB), RB)
                k.blk[at, :] = jnp.where(head == h, gm, 0.0).astype(bf16)
            by_gain = jnp.sum(gn * gated * rx, axis=0, keepdims=True)
            by_skip = jnp.sum(gm * k.X[l, r, :], axis=0, keepdims=True)
            return sums[0] + by_gain, sums[1] + by_skip

        zero = jnp.zeros((1, NC), f32)
        by_gain, by_skip = lax.fori_loop(
            0,
            T // RB,
            lambda i, s: gates(pl.ds(pl.multiple_of(i * RB, RB), RB), i, s),
            (zero, zero),
        )
        k.fpS[l] = jnp.zeros((24, 384), f32)
        k.fpS[l, 13:14, 0:NC] = by_gain
        k.fpS[l, 14:15, 0:NC] = by_skip
        k.stS[2 + l, 0:NC, :] = tn(k.eg[...], k.Cm[l]).astype(bf16)
        k.stS[2 + l, NC : NC + 16, :] = k.stS[l, NC : NC + 16, :]
        states = states_to(2 + l, True)
        dxt = jnp.zeros((T, NC), f32)
        for h in range(3):
            part = k.blk[h * T : h * T + T, :]
            dxt = dxt + tn(k.Wc[l, :, h * T : h * T + T], part)
            k.dW[h] = nt(part, k.xt[l])
        k.dxt[...] = dxt

        def pairs(r, i):
            g_sum = jnp.zeros((32, T), f32)
            for h in range(3):
                w = k.dW[h, r, :] * k.M[l, h, r, :]
                g_sum = g_sum + w
                k.Pb[h, r, :] = (w * k.G[l, r, :]).astype(bf16)
            k.dG[r, :] = g_sum.astype(bf16)

        over(T, 32, pairs)
        flow = jnp.zeros((8, T), f32)
        for h in range(3):
            one = ones_where(iota((8, T), 0) == h)
            flow = flow + nt(one, k.Pb[h]) - nn(one, k.Pb[h])
        meanwhile()
        both(states)
        after = joined(2 + l, True)
        through = after * k.s0[l]
        rows = [jnp.sum(through[HD * h : HD * h + HD], axis=0, keepdims=True) for h in range(3)]
        rows = jnp.concatenate(rows + [jnp.zeros((5, S), f32)], axis=0)
        constant = jnp.sum(rows * k.eT[l], axis=1, keepdims=True)
        after = after.astype(bf16)
        k.bes[...] = nt(k.Bm[l], after)
        k.dbc[:, 0:S] = tn(k.dG[...], k.Cm[l]) + nn(k.xtail[l], after)
        k.dbc[:, S:G2] = nn(k.dG[...], k.Bm[l]) + nn(k.eg[...], k.s0[l].astype(bf16))

        def inputs(r, i):
            x, gm, dte = k.X[l, r, :], k.gm[r, :], k.dte[l, r, :]
            tail = k.tl[l, r, :] * k.bes[r, :]
            dx = k.dxt[r, :] + tail
            k.qs[r, :] = (x * dte * tail).astype(bf16)
            k.gis[r, :] = (gm * k.yin[l, r, :]).astype(bf16)
            k.dds[r, :] = (dx * x).astype(bf16)
            v = k.va[l, r, :]
            s = sigmoid(v)
            k.ux[l, r, :] = (dte * dx + k.pk[l, 7:8, 0:NC] * gm) * (s * (1.0 + v * (1.0 - s)))
            v = k.vb[l, r, :]
            s = sigmoid(v)
            k.ub[l, r, :] = k.dbc[r, :] * (s * (1.0 + v * (1.0 - s)))

        over(T, RB, inputs)
        halo_x = op(k.ux.at[l, 0:8], k.ux.at[l, T : T + 8])
        halo_b = op(k.ub.at[l, 0:8], k.ub.at[l, T : T + 8])
        before = lax.rem(d + DP - 1, DP)
        halo_x.to(k.ux.at[l, 0:8], k.ux.at[l, T : T + 8], dp=before)
        halo_b.to(k.ub.at[l, 0:8], k.ub.at[l, T : T + 8], dp=before)
        q, inter = nt(per_head, k.qs[...]), nt(per_head, k.gis[...])
        direct = nt(per_head, k.dds[...])
        da = running(flow + inter, True) + (running(q) - q) + constant
        a_log = k.pk[l, 8:16, T : 2 * T]
        gdt = (direct - jnp.exp(a_log) * da) * k.sgd[l]
        k.gdt2[l, :, 0:T] = gdt
        k.fpS[l, 16:24, 0:128] = jnp.broadcast_to(jnp.sum(gdt, axis=1, keepdims=True), (8, 128))
        by_a = jnp.sum(k.arow[l] * da, axis=1, keepdims=True)
        k.fpS[l, 16:24, 128:256] = jnp.broadcast_to(by_a, (8, 128))
        halo_x.arrived()
        halo_b.arrived()

        def conv_back(u, ext, lane, width, dst):
            lanes = slice(lane, lane + width)

            def step(i, sums):
                near = pl.ds(pl.multiple_of(i * RB, RB), RB + 8)
                r = pl.ds(pl.multiple_of(i * RB, RB), RB)
                ublock, before = u[l, near, :], ext[l, near, :]
                g = k.pk[l, 4:5, lanes] * ublock[0:RB]
                here = ublock[0:RB]
                out = [
                    sums[0] + jnp.sum(here * before[8:], axis=0, keepdims=True),
                ]
                for lag in range(1, CONV):
                    masked = ublock * k.cmask[lag - 1, near, 0:width]
                    g = g + k.pk[l, 4 - lag : 5 - lag, lanes] * masked[lag : RB + lag]
                    moved = before[8 - lag : RB + 8 - lag]
                    out.append(
                        sums[lag] + jnp.sum(masked[0:RB] * moved, axis=0, keepdims=True)
                    )
                out.append(sums[CONV] + jnp.sum(here, axis=0, keepdims=True))
                dst[l, r, :] = g.astype(bf16)
                return tuple(out)

            zero = jnp.zeros((1, width), f32)
            return lax.fori_loop(0, T // RB, step, (zero,) * (CONV + 1))

        by_bc = conv_back(k.ub, k.be, 256, G2, k.gbp)
        bc = op(k.gbr.at[l], k.gbr.at[l])

        def give_bc(j, to):
            rows = pl.ds(pl.multiple_of(to * TB, TB), TB)
            bc.to(k.gbp.at[l, rows], k.gbr.at[l, j - 1], tensor=to)

        peers(give_bc)
        by_x = conv_back(k.ux, k.xe, 0, NC, k.gx2)
        k.gpS[l] = jnp.zeros((8, 384), f32)
        for lag in range(CONV):
            k.fpS[l, 8 + 3 - lag : 9 + 3 - lag, 0:NC] = by_x[lag]
            k.gpS[l, 4 + 3 - lag : 5 + 3 - lag, 0:G2] = by_bc[lag]
        k.fpS[l, 12:13, 0:NC] = by_x[CONV]
        k.gpS[l, 4:5, G2 : G2 + 128] = by_bc[CONV][:, 0:128]
        k.gpS[l, 5:6, G2 : G2 + 128] = by_bc[CONV][:, 128:256]
        gdt_cols = jnp.concatenate([gdt, jnp.zeros((120, T), f32)], axis=0).T.astype(bf16)
        for j in range(D // 256):
            at = slice(256 * j, 256 * j + 256)
            part = nn(k.gz2[l, 0:T, :], k.wz[l, :, at]) + nn(k.gx2[l, 0:T, :], k.wx[l, :, at])
            part = part + nt(k.gbp[l], k.wbc[l, at, :]) + nn(gdt_cols, k.wdt[l, :, at])
            k.us[2 + l, :, :, :, at] = part.astype(bf16).reshape(TZ, TX, TB, 256)
        return scatter(2 + l), bc

    def input_rows(l, made):
        gn = summed(made, 2 + l)
        h = k.hb[l, tz, tx].astype(f32)
        scale = lax.rsqrt(jnp.mean(h * h, axis=1, keepdims=True) + EPS)
        weighted = gn * k.pk[l, 0:1, :]
        inner = jnp.sum(weighted * h, axis=1, keepdims=True)
        gh = scale * weighted - h * (scale * scale * scale * (1.0 / D) * inner)
        low = (k.go2[l, 0, tz, tx].astype(f32) + gh).astype(bf16)
        by_pre = jnp.sum(gn * h * scale, axis=0, keepdims=True)
        for j in range(4):
            k.gpS[l, j : j + 1, :] = by_pre[:, 384 * j : 384 * j + 384]
        if l == 1:
            sums = jnp.sum(low.astype(f32) * k.u0[...], axis=1, keepdims=True)
            k.crossS[...] = jnp.broadcast_to(sums, (TB, 128))
        return low

    def operands(l):
        pairs = [(k.gz2.at[l, 0:T], k.gz2.at[l, T : 2 * T])]
        pairs += [(k.gx2.at[l, 0:T], k.gx2.at[l, T : 2 * T])]
        pairs += [(k.ni2.at[l, 0:T], k.ni2.at[l, T : 2 * T])]
        pairs += [(k.gdt2.at[l, :, 0:T], k.gdt2.at[l, :, T : 2 * T])]
        ops = [op(a, b, c != l, c == l) for a, b in pairs]

        @pl.when(c != l)
        def _():
            for made, (a, b) in zip(ops, pairs):
                made.to(a, b, pipe=other)

        return ops

    def bc_total(l, bc):
        bc.arrived()
        total = k.gbp[l, mine, :].astype(f32)
        for j in range(TP - 1):
            total = total + k.gbr[l, j].astype(f32)
        k.gbo[l] = total.astype(bf16)
        near = op(k.gb2.at[l, 0 : T - TB], k.gb2.at[l, 0 : T - TB], c == l, c == l)
        far = op(k.gb2.at[l, 0:T], k.gb2.at[l, 0:T], c != l, c == l)

        @pl.when(c == l)
        def _():
            peers(lambda j, to: near.to(k.gbo.at[l], k.gb2.at[l, mine], tensor=to))
            k.gb2[l, mine, :] = k.gbo[l]

        @pl.when(c != l)
        def _():
            there = pl.ds(pl.multiple_of(T + t * TB, TB), TB)
            peers(
                lambda j, to: far.to(k.gbo.at[l], k.gb2.at[l, there], pipe=other, tensor=to),
                0,
            )

        return near, far

    def ring(l, name, axis_rows):
        sent, recv = getattr(k, name + "S"), getattr(k, name + "R")
        made = op(recv.at[l], recv.at[l], c == l, c == l)

        def start():
            for j in range(1, DP):
                to = lax.rem(d + j, DP)
                rows = pl.ds(pl.multiple_of(to * axis_rows, axis_rows), axis_rows)
                made.to(sent.at[l, rows], recv.at[l, j - 1], dp=to)

        return made, start

    def ring_end(l, name, made, out, axis_rows):
        sent, recv, own = (getattr(k, name + x) for x in "SRO")
        rows = pl.ds(pl.multiple_of(d * axis_rows, axis_rows), axis_rows)
        total_rows = axis_rows * (DP - 1)
        spread = op(out.at[0, 0:total_rows], out.at[0, 0:total_rows], c == l, c == l)

        def finish():
            made.arrived()
            total = sent[l, rows, :].astype(f32)
            for j in range(DP - 1):
                total = total + recv[l, j].astype(f32)
            own[l] = total.astype(bf16)
            for j in range(1, DP):
                spread.to(own.at[l], out.at[0, rows], dp=lax.rem(d + j, DP))

        return spread, finish, (own.at[l], out.at[0, rows])

    def weight_grads(l, n_op, factor_ops, go_op):
        dz, start_z = ring(l, "dz", NC // DP)
        dx, start_x = ring(l, "dx", NC // DP)
        do, start_o = ring(l, "do", NC // DP)
        dt_made = op(k.dtR.at[l], k.dtR.at[l], c == l, c == l)

        @pl.when(c == l)
        def _():
            n_op.take()
            for made in factor_ops:
                made.take()
            if go_op is not None:
                go_op.take()
            for start, dst, left, right in (
                (start_x, k.dxS, k.gx2, k.n2),
                (start_z, k.dzS, k.gz2, k.n2),
                (start_o, k.doS, k.ni2, k.go2),
            ):
                for j in range(D // 256):
                    at = slice(256 * j, 256 * j + 256)
                    dst[l, :, at] = tn(left[l], right[l, ..., at].reshape(2 * T, 256)).astype(bf16)
                start()
            steps = jnp.concatenate([k.gdt2[l], jnp.zeros((8, 2 * T), f32)], axis=0).astype(bf16)
            k.dtS[l] = nn(steps, k.n2[l])[0:8]
            for j in range(1, DP):
                dt_made.to(k.dtS.at[l], k.dtR.at[l, j - 1], dp=lax.rem(d + j, DP))

        return dz, dx, do, dt_made

    def bc_grads(l, bc_ops):
        db_made = op(k.dbR.at[l], k.dbR.at[l], c == l, c == l)

        @pl.when(c == l)
        def _():
            for made in bc_ops:
                made.take()
            part = pl.ds(pl.multiple_of(lax.rem(t, slabs) * slab, slab), slab)
            k.dbS[l] = tn(k.n2[l, :, part], k.gb2[l]).astype(bf16)
            for j in range(1, DP):
                db_made.to(k.dbS.at[l], k.dbR.at[l, j - 1], dp=lax.rem(d + j, DP))

        return db_made

    def weight_ends(l, made):
        dz, dx, do, dt_made = made
        ends = [
            ring_end(l, "dx", dx, k.o_wx, NC // DP),
            ring_end(l, "dz", dz, k.o_wz, NC // DP),
            ring_end(l, "do", do, k.o_wout, NC // DP),
        ]

        @pl.when(c == l)
        def _():
            copies = []
            for i, (_, finish, (src, dst)) in enumerate(ends):
                finish()
                copies.append(local(src, dst, 12 + i))
                copies[-1].start()
            dt_made.arrived()
            total = k.dtS[l]
            for j in range(DP - 1):
                total = total + k.dtR[l, j]
            k.o_dt[...] = total
            for copy in copies:
                copy.wait()

        return [e[0] for e in ends]

    def bc_ends(l, db_made):
        rows = pl.ds(pl.multiple_of(lax.rem(t, slabs) * slab, slab), slab)
        owner, reader = (c == l) & (t < slabs), (c == l) & (t >= slabs)
        sent = k.n2.at[l, 0 : slab * (TP - 1) * G2 // D]
        from_rest = k.o_wbc.at[0, 0 : D - slab]
        spread = op(sent, from_rest, owner, owner)
        spread_all = spread.beside(k.o_wbc.at[0], reader)

        @pl.when(c == l)
        def _():
            db_made.arrived()
            total = k.dbS[l].astype(f32)
            for j in range(DP - 1):
                total = total + k.dbR[l, j].astype(f32)
            k.dbO[l] = total.astype(bf16)
            keep = local(k.dbO.at[l], k.o_wbc.at[0, rows], 15)

            @pl.when(t < slabs)
            def _():
                peers(lambda j, to: spread.to(k.dbO.at[l], k.o_wbc.at[0, rows], tensor=to))
                keep.start()
                keep.wait()

        return [spread, spread_all]

    def small_start(l):
        made = op(k.gpR.at[l], k.gpR.at[l])
        peers(lambda j, to: made.to(k.gpS.at[l], k.gpR.at[l, j - 1], tensor=to))
        return made

    def small_middle(l, made):
        made.arrived()
        total = k.gpS[l]
        for j in range(TP - 1):
            total = total + k.gpR[l, j]
        k.fpS[l, 0:8, :] = total
        near = op(k.fpR.at[l, 0 : DP - 1], k.fpR.at[l, 0 : DP - 1], c == l, c == l)
        far = op(k.fpR.at[l, DP - 1 :], k.fpR.at[l, DP - 1 :], c != l, c == l)

        @pl.when(c == l)
        def _():
            for j in range(1, DP):
                near.to(k.fpS.at[l], k.fpR.at[l, j - 1], dp=lax.rem(d + j, DP))

        @pl.when(c != l)
        def _():
            for j in range(DP):
                far.to(k.fpS.at[l], k.fpR.at[l, DP - 1 + j], pipe=other, dp=lax.rem(d + j, DP))

        return near, far

    def small_end(l, made):
        for m in made:
            m.arrived()

        @pl.when(c == l)
        def _():
            total = k.fpS[l]
            for j in range(2 * DP - 1):
                total = total + k.fpR[l, j]
            k.o_pack[...] = total

    in_tokens.wait()
    made, n_op0 = forward(0)
    made = scatter_on(0, made)
    rows = section_rows(0, made)
    made = gather_on(k.hb.at[1], gather(k.hb.at[1], rows))
    both(made)
    sec0, sec0_keep = hand_out(k.hb.at[1], k.o_sec, 0, 3)
    in_cot.wait()
    in_cot_other.wait()
    made1, n_op1 = forward(1)
    held_back = []
    made2, bc1 = backward(1, lambda: held_back.append(scatter_on(1, made1)))
    factors1 = operands(1)
    k.own[1] = section_rows(1, held_back[0])
    grads1 = weight_grads(1, n_op1, factors1, None)
    made2 = scatter_on(3, made2)
    bc_ops1 = bc_total(1, bc1)
    rows = input_rows(1, made2)
    made2 = gather(k.go2.at[0, 0], rows)
    cross = op(k.cross.at[0 : T - TB], k.cross.at[0 : T - TB])
    peers(lambda j, to: cross.to(k.crossS, k.cross.at[mine], tensor=to))
    k.cross[mine, :] = k.crossS[...]
    made2 = gather_on(k.go2.at[0, 0], made2)
    small1 = small_start(1)
    db1 = bc_grads(1, bc_ops1)
    both(made2)
    cross.arrived()
    ing1, ing1_keep = hand_out(k.go2.at[0, 0], k.o_ing, 1, 4)
    go_op = op(k.go2.at[0, 0], k.go2.at[0, 1], c != 0, c == 0)
    pl.when(c != 0)(lambda: go_op.to(k.go2.at[0, 0], k.go2.at[0, 1], pipe=other))
    sec1 = spread(k.own.at[1], k.o_sec, 1, 9)
    made3, bc0 = backward(0, lambda: held_back.append(spread_on(k.o_sec, 1, sec1)))
    factors0 = operands(0)
    grads0 = weight_grads(0, n_op0, factors0, go_op)
    made3 = scatter_on(2, made3)
    bc_ops0 = bc_total(0, bc0)
    packs1 = small_middle(1, small1)
    spreads = weight_ends(1, grads1)
    k.own[0] = input_rows(0, made3)
    ing0 = spread(k.own.at[0], k.o_ing, 0, 8)
    small0 = small_start(0)
    db0 = bc_grads(0, bc_ops0)
    spreads += weight_ends(0, grads0)
    ing0 = spread_on(k.o_ing, 0, ing0)
    spreads += bc_ends(1, db1)
    packs0 = small_middle(0, small0)
    spreads += bc_ends(0, db0)
    small_end(1, packs1)
    small_end(0, packs0)
    sec0.arrived()
    sec0_keep()
    ing1.arrived()
    ing1_keep()
    both(held_back[1])
    both(ing0)
    both(spreads)
    for copy in w_sent:
        copy.wait_send()
    for made in pending:
        made.left()


def finish(geo, sec, ing, dz, dx, dbc, do, dt, pack, *outs):
    T, D, NC, S = geo
    G2 = 2 * S
    o_sec, o_ing, o_pre, o_z, o_x, o_bc, o_dt, o_cx, o_cbc, o_bx, o_bbc, o_dtb = outs[:12]
    o_alog, o_dsk, o_gain, o_out, sems = outs[12:]
    copies = [
        pltpu.make_async_copy(sec, o_sec, sems.at[0]),
        pltpu.make_async_copy(ing, o_ing, sems.at[1]),
    ]
    for copy in copies:
        copy.start()
    for src, dst, rows in ((dz, o_z, NC), (dx, o_x, NC), (do, o_out, NC), (dbc, o_bc, D)):

        def widen(r, i, src=src, dst=dst):
            dst[0, r, :] = src[0, r, :].astype(f32)

        over(rows, 32, widen)
    for j in range(4):
        o_pre[:, 384 * j : 384 * j + 384] = pack[j : j + 1, :]
    for h in range(o_dt.shape[0]):
        o_dt[h] = dt[h : h + 1, :]
    o_cx[0] = pack[8:12, 0:NC]
    o_cbc[0] = pack[4:8, 0:G2]
    o_bx[...] = pack[12:13, 0:NC]
    o_bbc[:, 0:128] = pack[4:5, 256:384]
    o_bbc[:, 128:256] = pack[5:6, 256:384]
    o_gain[...] = pack[13:14, 0:NC]
    lane = iota((1, 3), 1)
    chan = iota((1, NC), 1)
    b, a, s = (jnp.zeros((1, 3), f32),) * 3
    for h in range(3):
        one = lane == h
        b = jnp.where(one, pack[16 + h : 17 + h, 0:1], b)
        a = jnp.where(one, pack[16 + h : 17 + h, 128:129], a)
        by_skip = jnp.where(chan // HD == h, pack[14:15, 0:NC], 0.0)
        s = jnp.where(one, jnp.sum(by_skip, axis=1, keepdims=True), s)
    o_dtb[...], o_alog[...], o_dsk[...] = b, a, s
    for copy in copies:
        copy.wait()


def on_device(sizes, *args):
    (tokens, seq, cot, pre, wz, wx, wbc, wdt, cx, cbc, bx, bbc, dtb, alog, dsk, gain, wout) = args
    (TZ, TX), DP = sizes
    _, T, D = tokens.shape
    TB = T // (TZ * TX)
    NC, S = wx.shape[2], wbc.shape[2] // 2
    wdt = jnp.pad(jnp.swapaxes(wdt, 1, 2), ((0, 0), (0, 13), (0, 0)))
    wz, wx = jnp.swapaxes(wz, 1, 2), jnp.swapaxes(wx, 1, 2)
    tokens, cot = (x.reshape(2, TZ, TX, TB, D) for x in (tokens, cot))
    scratch = scratch_of(T, D, NC, S, TZ, TX, DP)
    names = tuple(INPUTS) + tuple(OUTPUTS) + tuple(scratch)
    any_, vmem, smem = (pl.BlockSpec(memory_space=m) for m in (pl.ANY, pltpu.VMEM, pltpu.SMEM))
    made = pl.pallas_call(
        functools.partial(kernel, (T, D, NC, S, TZ, TX, DP), names),
        out_shape=(
            jax.ShapeDtypeStruct((1, 2, TZ, TX, TB, D), bf16),
            jax.ShapeDtypeStruct((1, 2, TZ, TX, TB, D), bf16),
            jax.ShapeDtypeStruct((1, NC, D), bf16),
            jax.ShapeDtypeStruct((1, NC, D), bf16),
            jax.ShapeDtypeStruct((1, D, 2 * S), bf16),
            jax.ShapeDtypeStruct((1, NC, D), bf16),
            jax.ShapeDtypeStruct((8, D), f32),
            jax.ShapeDtypeStruct((24, 384), f32),
        ),
        in_specs=[any_] * 7 + [vmem] * 6 + [smem] * 4,
        out_specs=(any_,) * 6 + (vmem,) * 2,
        scratch_shapes=list(scratch.values()),
        compiler_params=pltpu.CompilerParams(
            collective_id=0, has_side_effects=True, vmem_limit_bytes=60 * 1024 * 1024
        ),
    )(tokens, cot, wz, wx, wbc, wdt, wout, pre, cx, cbc, bx, bbc, gain, seq, dtb, alog, dsk)
    heads = NC // HD
    done = pl.pallas_call(
        functools.partial(finish, (T, D, NC, S)),
        out_shape=(
            jax.ShapeDtypeStruct((1, 2, TZ, TX, TB, D), bf16),
            jax.ShapeDtypeStruct((1, 2, TZ, TX, TB, D), bf16),
            jax.ShapeDtypeStruct((1, D), f32),
            jax.ShapeDtypeStruct((1, NC, D), f32),
            jax.ShapeDtypeStruct((1, NC, D), f32),
            jax.ShapeDtypeStruct((1, D, 2 * S), f32),
            jax.ShapeDtypeStruct((heads, 1, D), f32),
            jax.ShapeDtypeStruct((1, CONV, NC), f32),
            jax.ShapeDtypeStruct((1, CONV, 2 * S), f32),
            jax.ShapeDtypeStruct((1, NC), f32),
            jax.ShapeDtypeStruct((1, 2 * S), f32),
            jax.ShapeDtypeStruct((1, heads), f32),
            jax.ShapeDtypeStruct((1, heads), f32),
            jax.ShapeDtypeStruct((1, heads), f32),
            jax.ShapeDtypeStruct((1, NC), f32),
            jax.ShapeDtypeStruct((1, NC, D), f32),
        ),
        in_specs=[any_] * 2 + [vmem] * 6,
        out_specs=(any_,) * 2 + (vmem,) * 14,
        scratch_shapes=[pltpu.SemaphoreType.DMA((2,))],
        compiler_params=pltpu.CompilerParams(vmem_limit_bytes=40 * 1024 * 1024),
    )(*made)
    swap = {3: (0, 2, 1), 4: (0, 2, 1), 6: (1, 2, 0)}
    done = [x.reshape(1, 2, T, D) for x in done[:2]] + list(done[2:])
    return tuple(jnp.transpose(x, swap[i]) if i in swap else x for i, x in enumerate(done))


def solution(mesh):
    side = int(mesh.shape["tensor"] ** 0.5)
    split = (side, mesh.shape["tensor"] // side)
    in_specs = (
        P(None, "dp", None),
        P(),
        P(None, "dp", None),
        P("pipe", None),
        P("pipe", None, "tensor"),
        P("pipe", None, "tensor"),
        P("pipe", None, None),
        P("pipe", None, "tensor"),
        P("pipe", None, "tensor"),
        P("pipe", None, None),
        P("pipe", "tensor"),
        P("pipe", None),
        P("pipe", "tensor"),
        P("pipe", "tensor"),
        P("pipe", "tensor"),
        P("pipe", "tensor"),
        P("pipe", "tensor", None),
    )
    out_specs = (
        P("pipe", None, "dp", None),
        P("pipe", None, "dp", None),
        P("pipe", None),
        P("pipe", None, "tensor"),
        P("pipe", None, "tensor"),
        P("pipe", None, None),
        P("pipe", None, "tensor"),
        P("pipe", None, "tensor"),
        P("pipe", None, None),
        P("pipe", "tensor"),
        P("pipe", None),
        P("pipe", "tensor"),
        P("pipe", "tensor"),
        P("pipe", "tensor"),
        P("pipe", "tensor"),
        P("pipe", "tensor", None),
    )
    return jax.shard_map(
        functools.partial(on_device, (split, mesh.shape["dp"])),
        mesh=mesh,
        in_specs=in_specs,
        out_specs=out_specs,
        check_vma=False,
    )
```
